512 devices in a mesh: gx: 32 (over z_lo, x), gy: 16 (over z_hi, y, core).
Axes of the slice: x: 4, y: 4, z: 16 (z_hi: 2, z_lo: 8; z = z_hi * 8 + z_lo), core: 2. Of those that a mesh axis runs over, the one named last changes fastest.
Arguments:
- displacement: float32 [3, 128, 128, 128], P(None, 'gx', 'gy'), may hold values from -0.15 to 0.15
- velocity: float32 [3, 128, 128, 128], P(None, 'gx', 'gy'), may hold values from -4 to 4
- stiffness: float32 [128, 128, 128], P('gx', 'gy'), may hold values from 0.5 to 4
- damage: int32 [6, 128, 128, 128], P(None, 'gx', 'gy'), may hold values from 0 to 2047, as said below
Outputs:
- new_displacement: float32 [3, 128, 128, 128], P(None, 'gx', 'gy')
- new_velocity: float32 [3, 128, 128, 128], P(None, 'gx', 'gy')
The draws below stay inside these ranges and needn't reach their ends.
Inputs may be any that keep to these rules, and one draw needn't show every extreme that they name: `damage`: bits above bit 10 are zero; in the last word only bits 0 to 5 are used.
All inputs are finite; a program needn't handle non-finite values.
Results may differ from the reference program's by a relative error of at most 0.0001.
Values sent between devices are 32-bit elements; how exact they have to be, the bound alone decides.
No kernel may reach another device: no remote copies, remote signals or barrier semaphores. Data moves between devices by JAX's collectives and lax.ppermute only.
A program may use at most 64 MiB of HBM per device.

```python
import math
import jax
import jax.numpy as jnp
from jax import lax

NZ = 128
STEPS = 2
WORDS = 6
NX = 128
NY = 128


def draw_damage(key, part):
    key = jax.random.fold_in(key, 11)
    limits = jnp.array([2048, 2048, 2048, 2048, 2048, 64], jnp.int32).reshape(6, 1, 1, 1)
    return jax.random.randint(key, (WORDS, NX, NY, NZ), 0, limits, dtype=jnp.int32)


def block_scale(key, shape, split, smallest, high):
    gain = 1.0
    for position, shards_of in split:
        draws = jax.random.uniform(jax.random.fold_in(jax.random.fold_in(key, 6), position), (shards_of,), jnp.float32, smallest / len(split), high / len(split))
        gain = gain * jnp.repeat(jnp.exp(draws), shape[position] // shards_of).reshape((-1,) + (1,) * (len(shape) - 1 - position))
    return gain


def centred(stream_key, dims, spread, reach, shards=(), kind=jnp.bfloat16):
    level = block_scale(stream_key, dims, shards, -0.22, 0.18) if shards else 1.0
    result = jax.random.normal(stream_key, dims, jnp.float32) * spread * level
    return jnp.minimum(jnp.maximum(result, -reach), reach).astype(kind)


def setup_inputs(seed: int = 0) -> dict:
    key_of = jax.random.split(jax.random.key(seed), 5)
    return {
        "displacement": centred(key_of[0], (3, NX, NY, NZ), 0.05, 0.15, ((1, 32), (2, 16)), jnp.float32),
        "velocity": centred(key_of[1], (3, NX, NY, NZ), 1.0, 4.0, ((1, 32), (2, 16)), jnp.float32),
        "stiffness": jnp.clip(jnp.exp(math.log(4.0) - 2.0794415 * jax.random.uniform(key_of[2], (NX, NY, NZ), jnp.float32) ** block_scale(key_of[2], (NX, NY, NZ), ((0, 32), (1, 16)), -0.2, 0.2)), 0.5, 4.0),
        "damage": draw_damage(jax.random.fold_in(key_of[4], 71), 0),
    }


time_step = 0.02
bond_scale = 100.0

def bond_offsets():
    table = []
    for step_x in range(0, 4):
        for step_y in range(-3, 4):
            for step_z in range(-3, 4):
                if step_x * step_x + step_y * step_y + step_z * step_z <= 9 and (step_x, step_y, step_z) > (0, 0, 0):
                    table.append((step_x, step_y, step_z))
    return table

def bond_force(center, neighbour, center_k, neighbour_k, broken, offset):
    length = math.sqrt(offset[0] ** 2 + offset[1] ** 2 + offset[2] ** 2)
    shift_vec = jnp.array(offset, jnp.float32).reshape(3, 1, 1, 1)
    separation = neighbour - center + shift_vec
    distance = jnp.sqrt(lax.optimization_barrier(jnp.sum(separation * separation, axis=0)))
    factor = bond_scale * jnp.sqrt(center_k * neighbour_k) * (1.0 - broken) * (distance - length) / (length * distance)
    return factor[None] * separation

def broken_bits(damage, index):
    damage_word = damage[index // 11]
    return jnp.bitwise_and(jnp.right_shift(damage_word, index % 11), 1).astype(jnp.float32)

def total_force(displacement, stiffness, damage):
    padded_u = jnp.pad(displacement, ((0, 0), (3, 3), (3, 3), (3, 3)))
    padded_k = jnp.pad(stiffness, 3)
    owned = jnp.zeros((3, NX, NY, NZ), jnp.float32)
    reaction = jnp.zeros((3, NX + 6, NY + 6, NZ + 6), jnp.float32)
    for index, offset in enumerate(bond_offsets()):
        step_x, step_y, step_z = offset
        neighbour = padded_u[:, 3 + step_x:3 + step_x + NX, 3 + step_y:3 + step_y + NY, 3 + step_z:3 + step_z + NZ]
        neighbour_k = padded_k[3 + step_x:3 + step_x + NX, 3 + step_y:3 + step_y + NY, 3 + step_z:3 + step_z + NZ]
        force = bond_force(displacement, neighbour, stiffness, neighbour_k, broken_bits(damage, index), offset)
        owned = owned + force
        reaction = reaction - jnp.pad(force, ((0, 0), (3 + step_x, 3 - step_x), (3 + step_y, 3 - step_y), (3 + step_z, 3 - step_z)))
    return owned + reaction[:, 3:3 + NX, 3:3 + NY, 3:3 + NZ]

def reference(displacement, velocity, stiffness, damage):
    for iteration in range(STEPS):
        force = total_force(displacement, stiffness, damage)
        velocity = velocity + time_step * force
        displacement = displacement + time_step * velocity
    return (displacement, velocity)
```

```python
import math

import jax
import jax.numpy as jnp
from jax import lax
from jax.experimental import pallas as pl
from jax.experimental.pallas import tpu as pltpu
from jax.sharding import PartitionSpec as P

STEPS = 2

time_step = 0.02
bond_scale = 100.0

PLANES, ROWS = 10, 16
LOW = 3
V, K, D, FIELD_COUNT = 3, 6, 7, 13
ROLLS = (-2, -1, 1, 2)


def bond_offsets():
    table = []
    for step_x in range(0, 4):
        for step_y in range(-3, 4):
            for step_z in range(-3, 4):
                if step_x * step_x + step_y * step_y + step_z * step_z <= 9 and (
                    step_x,
                    step_y,
                    step_z,
                ) > (0, 0, 0):
                    table.append((step_x, step_y, step_z))
    return table


BONDS = list(enumerate(bond_offsets()))

RIGHT_WORDS = [(3, 2, w) for w in range(1, 6)] + [(2, 1, w) for w in range(3, 6)] + [(1, 0, 5)]


def y_slots(upward):
    slots = []
    place = 0

    def put(kind, comp, depth, plane, count):
        nonlocal place
        here = LOW + 7 - depth if upward else LOW + depth
        there = LOW - 1 - depth if upward else LOW + 8 + depth
        slots.append((kind, comp, here, there, plane, count, place))
        place += count

    for kind, comps in (("u", 3), ("s", 1)):
        for comp in range(comps):
            for depth in range(3):
                put(kind, comp, depth, *((1, 8) if depth < 2 else (3, 4)))
    for comp in range(3):
        for depth in range(3):
            put("d", comp, depth, 3, 4)
    words = ((0, 1, 2, 3, 4, 5), (0, 1, 3, 5), (1,)) if upward else ((1, 2, 3, 4), (1, 3))
    for depth, row_words in enumerate(words):
        for word in row_words:
            put("w", word, depth, *((3, 4) if upward and word < 2 else (1, 6)))
    return slots, place


UP_SLOTS, UP_ROWS = y_slots(True)
DOWN_SLOTS, DOWN_ROWS = y_slots(False)
Y_ROWS = -(-max(UP_ROWS, DOWN_ROWS) // 8) * 8

CORNER_ROWS = (1, 2, 11, 12)


def line_of(row):
    return {0: 0, 1: 1, 2: 2, 11: 3, 12: 4, 13: 5, 3: 0, 4: 1, 5: 2, 8: 3, 9: 4, 10: 5}[row]


def spot(ref, plane, row, count=8):
    if ref.shape[-2] == ROWS:
        return (plane, slice(row, row + count))
    return (slice(plane * ROWS + row, plane * ROWS + row + count),)


def rolled(value, distance):
    return pltpu.roll(value, (-distance) % 128, value.ndim - 1)


def lane_mask(distance):
    lane = lax.broadcasted_iota(jnp.int32, (8, 128), 1)
    return lane < 128 - distance if distance > 0 else lane >= -distance


def roll_field(source, target, planes, halves=(0, 8)):
    for c in range(3):
        for plane in planes:
            for half in halves:
                value = source[(c,) + spot(source, plane, half)]
                for i, ez in enumerate(ROLLS):
                    target[(c, i) + spot(target, plane, half)] = rolled(value, ez)


def roll_stiffness(source, target, planes, halves=(0, 8)):
    for plane in planes:
        for half in halves:
            value = source[spot(source, plane, half)]
            for i, ez in enumerate(ROLLS):
                moved = jnp.where(lane_mask(ez), rolled(value, ez), 0.0)
                target[(i,) + spot(target, plane, half)] = moved


def add_bond(total, source, target, length, weight):
    sep = [a - b for a, b in zip(source, target)]
    square = sep[0] * sep[0] + sep[1] * sep[1] + sep[2] * sep[2]
    factor = (1.0 / length - lax.rsqrt(square)) * weight
    return [t + factor * p for t, p in zip(total, sep)]


def intact(q, words, value):
    return jnp.where(jnp.bitwise_and(words, 1 << (q % 11)) == 0, value, 0.0)


def rolled_back(part, ez):
    mask = lane_mask(-ez)
    return [jnp.where(mask, rolled(p, -ez), 0.0) for p in part]


def accumulate(plane, base, owned, reacted, u, ur, s, sr, d):
    here = [u[(c,) + spot(u, plane, base)] for c in range(3)]
    total = [jnp.zeros((8, 128), jnp.float32) for _ in range(3)]

    for ez in range(-3, 4):
        for q, (ex, ey, _) in [b for b in owned if b[1][2] == ez]:
            row, at = base + ey, plane + ex
            length = math.sqrt(ex * ex + ey * ey + ez * ez)
            if ez == 0:
                source = [u[(c,) + spot(u, at, row)] for c in range(3)]
                stiff = s[spot(s, at, row)]
            elif abs(ez) < 3:
                i = ROLLS.index(ez)
                source = [ur[(c, i) + spot(ur, at, row)] for c in range(3)]
                stiff = sr[(i,) + spot(sr, at, row)]
            else:
                source = [rolled(h, ez) for h in here]
                stiff = jnp.where(lane_mask(ez), rolled(s[spot(s, at, row)], ez), 0.0)
            target = [h - float(e) for h, e in zip(here, (ex, ey, ez))]
            words = d[(q // 11,) + spot(d, plane, base)]
            total = add_bond(total, source, target, length, intact(q, words, stiff))
        bonds = [b for b in reacted if b[1][2] == ez]
        if not bonds:
            continue
        moved = here if ez == 0 else [rolled(h, ez) for h in here]
        part = total if ez == 0 else [jnp.zeros((8, 128), jnp.float32) for _ in range(3)]
        for q, (ex, ey, _) in bonds:
            row, at = base - ey, plane - ex
            length = math.sqrt(ex * ex + ey * ey + ez * ez)
            source = [u[(c,) + spot(u, at, row)] for c in range(3)]
            target = [h + float(e) for h, e in zip(moved, (ex, ey, ez))]
            stiff = s[spot(s, at, row)]
            words = d[(q // 11,) + spot(d, at, row)]
            part = add_bond(part, source, target, length, intact(q, words, stiff))
        if ez == 0:
            total = part
        else:
            total = [t + p for t, p in zip(total, rolled_back(part, ez))]
    return total


def accumulate_row(row, sources, u, d, other):
    ou, our, os, osr, od, odr = other

    def line(plain, turned, lead, ez, plane, at):
        ref, lead = (plain, lead) if ez == 0 else (turned, lead + (ROLLS.index(ez),))
        return ref[lead + (line_of(at), slice(plane, plane + 8))]

    here = [u[c, line_of(row), 2:10] for c in range(3)]
    total = [jnp.zeros((8, 128), jnp.float32) for _ in range(3)]
    for q, bond in BONDS:
        length = math.sqrt(sum(e * e for e in bond))
        for sign in (1, -1):
            ex, ey, ez = (sign * e for e in bond)
            if row + ey not in sources:
                continue
            plane, at = 2 + ex, row + ey
            source = [line(ou, our, (c,), ez, plane, at) for c in range(3)]
            stiff = line(os, osr, (), ez, plane, at)
            if sign > 0:
                word = d[q // 11, line_of(row), 2:10]
            else:
                word = line(od, odr, (q // 11,), ez, plane, at)
            target = [h - float(e) for h, e in zip(here, (ex, ey, ez))]
            total = add_bond(total, source, target, length, intact(q, word, stiff))
    return [part[0:4] for part in total]


def put_own(fields, u, s, d):
    for x in range(4):
        if u is not None:
            for c in range(3):
                u[(c,) + spot(u, x + 3, LOW)] = fields[c, x]
        if s is not None:
            s[spot(s, x + 3, LOW)] = jnp.sqrt(fields[K, x])
        for w in range(6):
            d[(w,) + spot(d, x + 3, LOW)] = fields[D + w, x].astype(jnp.int32)


def put_zeros(ref, leads, planes, row, count):
    for lead in leads:
        for plane in planes:
            ref[lead + spot(ref, plane, row, count)] = jnp.zeros((count, 128), ref.dtype)


def put_sides(even, near, far, u, s, d):
    rows = slice(LOW, LOW + 8)

    def left(i):
        return jnp.where(even, far[i], near[i])

    def right(i):
        return jnp.where(even, near[i], far[i])

    for plane in range(3):
        for c in range(3):
            if u is not None:
                u[(c,) + spot(u, plane, LOW)] = left(3 * c + plane)
                u[(c,) + spot(u, 7 + plane, LOW)] = right(3 * c + plane)
        s[spot(s, plane, LOW)] = jnp.sqrt(left(9 + plane))
        s[spot(s, 7 + plane, LOW)] = jnp.sqrt(right(9 + plane))
    for i, (_, plane, word) in enumerate(RIGHT_WORDS):
        d[(word,) + spot(d, plane, LOW)] = left(12 + i).astype(jnp.int32)


def message_lines(even, a, b):
    for slots, above in ((DOWN_SLOTS, True), (UP_SLOTS, False)):
        for slot in slots:
            place, count = slot[6], slot[5]
            one, two = a[place : place + count], b[place : place + count]
            yield slot, jnp.where(even, one, two) if above else jnp.where(even, two, one)


def put_lines(even, a, b, u, s, d, edge):
    for (kind, comp, _, there, plane, count, _), value in message_lines(even, a, b):
        at, planes = line_of(there), slice(plane - 1, plane - 1 + count)
        if kind == "u":
            u[comp, at, planes] = value
        elif kind == "s":
            s[at, planes] = value
        elif kind == "d":
            edge[comp, at, 0:4] = value
        else:
            d[comp, at, planes] = value.astype(jnp.int32)


def put_rows(even, a, b, s, d, wanted):
    for (kind, comp, _, there, plane, count, _), value in message_lines(even, a, b):
        for i in range(count):
            if (plane + i in wanted) and kind == "s":
                s[spot(s, plane + i, there, 1)] = value[i : i + 1]
            elif (plane + i in wanted) and kind == "w":
                d[(comp,) + spot(d, plane + i, there, 1)] = value[i : i + 1].astype(jnp.int32)


def even_place():
    return tuple(lax.axis_index(axis) % 2 == 0 for axis in ("gx", "gy"))


def joined_fields(displacement, velocity, stiffness, damage):
    parts = (displacement, velocity, stiffness[None], damage.astype(jnp.float32))
    total, before = 0.0, 0
    for part in parts:
        count = part.shape[0]
        widths = ((before, FIELD_COUNT - before - count, 0),) + ((0, 0, 0),) * 3
        total = total + lax.pad(part, jnp.float32(0), widths)
        before += count
    return total


def pack_x(fields, far, near):
    even, _ = even_place()
    for i, field in enumerate((0, 1, 2, K)):
        for plane in range(3):
            one, two = fields[field, plane + 1], fields[field, plane]
            near[3 * i + plane] = jnp.where(even, one, two)
            far[3 * i + plane] = jnp.where(even, two, one)
    for i, (plane, _, word) in enumerate(RIGHT_WORDS):
        near[12 + i] = fields[D + word, plane]
        far[12 + i] = fields[D + word, plane]


SIDES = (0, 1, 2, 7, 8, 9)
OUTER = ((0, LOW), (LOW + 8, ROWS - LOW - 8))
EACH = ((0,), (1,), (2,))


def own_part(u, ur, s, sr, d, force):
    roll_field(u, ur, range(3, 7))
    roll_stiffness(s, sr, range(3, 7))
    for i in range(4):
        for plane in (7, 8):
            put_zeros(ur, [(c, i) for c in range(3)], (plane,), 0, ROWS)
            put_zeros(sr, [(i,)], (plane,), 0, ROWS)

    @pl.loop(0, 4)
    def _(x):
        total = accumulate(x + 3, LOW, BONDS, BONDS, u, ur, s, sr, d)
        for c in range(3):
            force[c, x] = total[c]


def side_part(x, u, ur, s, sr, d):
    owned = [b for b in BONDS if x + b[1][0] > 3]
    reacted = [b for b in BONDS if x - b[1][0] < 0]
    return accumulate(x + 3, LOW, owned, reacted, u, ur, s, sr, d)


def first_own(fields, force, u, ur, s, sr, d):
    put_zeros(u, EACH, SIDES, 0, ROWS)
    put_zeros(s, [()], SIDES, 0, ROWS)
    for row, count in OUTER:
        put_zeros(u, EACH, range(3, 7), row, count)
        put_zeros(s, [()], range(3, 7), row, count)
        put_zeros(d, [(w,) for w in range(6)], range(3, 7), row, count)
    put_own(fields, u, s, d)
    own_part(u, ur, s, sr, d, force)


def first_sides(fields, far_x, near_x, force, b, a, v_part, u, ur, s, sr, d, near, up, down):
    even_x, even = even_place()
    for row, count in OUTER:
        put_zeros(u, EACH, SIDES, row, count)
        put_zeros(s, [()], SIDES, row, count)
    put_own(fields, u, s, d)
    put_sides(even_x, near_x, far_x, u, s, d)
    roll_field(u, ur, (7, 8))
    roll_stiffness(s, sr, (7, 8))
    for x in range(4):
        total = side_part(x, u, ur, s, sr, d)
        scale = bond_scale * s[spot(s, x + 3, LOW)]
        for c in range(3):
            velocity = fields[V + c, x] + time_step * (scale * (force[c, x] + total[c]))
            v_part[c, x] = velocity
            near[(c,) + spot(u, x + 3, LOW)] = fields[c, x] + time_step * velocity

    for slots, message in ((UP_SLOTS, up), (DOWN_SLOTS, down)):
        for kind, comp, here, _, plane, count, place in slots:
            lines = pl.ds(plane * ROWS + here, count, stride=ROWS)
            if kind == "u":
                value = u[comp, lines]
            elif kind == "s":
                value = s[lines]
            elif kind == "d":
                value = near[comp, lines]
            else:
                value = d[comp, lines].astype(jnp.float32)
            message[place : place + count] = value
    a[...] = jnp.where(even, up[...], down[...])
    b[...] = jnp.where(even, down[...], up[...])


def roll_lines(u, ur, s, sr, d, dr, words):
    for at in range(6):
        for i, ez in enumerate(ROLLS):
            for w in words[at]:
                dr[w, i, at, 0:8] = rolled(d[w, at, 0:8], ez)
            for c in range(3):
                ur[c, i, at, 0:8] = rolled(u[c, at, 0:8], ez)
            sr[i, at, 0:8] = jnp.where(lane_mask(ez), rolled(s[at, 0:8], ez), 0.0)


def second_own(fields, far_x, near_x, u, ur, s, sr, d, dr, whole_u, whole_s, whole_d):
    even_x, _ = even_place()
    put_own(fields, whole_u, whole_s, whole_d)
    put_sides(even_x, near_x, far_x, whole_u, whole_s, whole_d)
    for row in (3, 4, 5, 8, 9, 10):
        at, lines = line_of(row), pl.ds(ROWS + row, 8, stride=ROWS)
        for c in range(3):
            u[c, at, 0:8] = whole_u[c, lines]
        s[at, 0:8] = whole_s[lines]
        for w in range(6):
            d[w, at, 0:8] = whole_d[w, lines]
    roll_lines(u, ur, s, sr, d, dr, [range(6)] * 6)


def second_rows(fields, b, a, v_part, u, ur, s, sr, d, dr, v_out, near, edge, to_far, to_near, hu, hur, hs, hsr, hd, hdr, sums):
    even_x, even = even_place()
    put_lines(even, a, b, hu, hs, hd, edge)
    sent = UP_SLOTS + DOWN_SLOTS
    words = [[k[1] for k in sent if k[0] == "w" and line_of(k[3]) == at] for at in range(6)]
    roll_lines(hu, hur, hs, hsr, hd, hdr, words)
    beside = (u, ur, s, sr, d, dr)
    beyond = (hu, hur, hs, hsr, hd, hdr)
    for row in (3, 4, 5, 8, 9, 10):
        sources = range(0, LOW) if row < LOW + 4 else range(LOW + 8, LOW + 11)
        force = accumulate_row(row, sources, u, d, beyond)
        for c in range(3):
            sums[c, 8 * (row - LOW) : 8 * (row - LOW) + 4] = force[c]
    for c in range(3):
        for row in (6, 7):
            sums[c, 8 * (row - LOW) : 8 * (row - LOW) + 8] = jnp.zeros((8, 128), jnp.float32)
    for row in (0, 1, 2, 11, 12, 13):
        sources = range(LOW, LOW + 3) if row < LOW + 4 else range(LOW + 5, LOW + 8)
        force = accumulate_row(row, sources, hu, hd, beside)
        at = line_of(row)
        scale = (time_step * time_step * bond_scale) * hs[at, 2:6]
        for c in range(3):
            edge[c, at, 0:4] += scale * force[c]
    for x in range(4):
        scale = (time_step * bond_scale) * jnp.sqrt(fields[K, x])
        for c in range(3):
            velocity = v_part[c, x] + scale * sums[c, pl.ds(x, 8, stride=8)]
            v_out[c, x] = velocity
            near[c, x] = fields[c, x] + time_step * velocity

    place = 0
    for c in range(3):
        for plane in range(3):
            one, two = near[c, plane + 1], near[c, plane]
            to_near[place : place + 8] = jnp.where(even_x, one, two)
            to_far[place : place + 8] = jnp.where(even_x, two, one)
            place += 8
    for c in range(3):
        for row in CORNER_ROWS:
            one, two = edge[c, line_of(row), 2:4], edge[c, line_of(row), 0:2]
            to_near[place : place + 2] = jnp.where(even_x, one, two)
            to_far[place : place + 2] = jnp.where(even_x, two, one)
            place += 2


def last_own(fields, far_x, near_x, b, a, near, edge, force, s, sr, d, u, ur):
    even_x, even = even_place()
    put_zeros(u, EACH, SIDES, 0, ROWS)
    put_zeros(s, [()], SIDES, 0, ROWS)
    put_own(fields, None, s, d)
    put_rows(even, a, b, s, d, range(3, 7))
    for c in range(3):
        u[c, 3:7, LOW : LOW + 8] = near[c]
        for row in (0, 1, 2, 11, 12, 13):
            for x in range(4):
                u[c, x + 3, row : row + 1] = edge[c, line_of(row), x : x + 1]
    own_part(u, ur, s, sr, d, force)
    put_sides(even_x, near_x, far_x, None, s, d)
    put_rows(even, a, b, s, d, SIDES)
    roll_stiffness(s, sr, (7, 8))


def last_sides(near, v_in, force, s, sr, d, far_u, near_u, u_out, v_out, u, ur):
    even_x, _ = even_place()
    for c in range(3):
        u[c, 3:7, LOW : LOW + 8] = near[c]
    put_zeros(u, EACH, SIDES, 0, LOW)
    put_zeros(u, EACH, SIDES, LOW + 8, ROWS - LOW - 8)
    place = 0
    for c in range(3):
        for plane in range(3):
            one, two = near_u[place : place + 8], far_u[place : place + 8]
            u[c, plane, LOW : LOW + 8] = jnp.where(even_x, two, one)
            u[c, 7 + plane, LOW : LOW + 8] = jnp.where(even_x, one, two)
            place += 8
    for c in range(3):
        for row in CORNER_ROWS:
            one, two = near_u[place : place + 2], far_u[place : place + 2]
            before, behind = jnp.where(even_x, two, one), jnp.where(even_x, one, two)
            for plane in range(2):
                u[c, 1 + plane, row : row + 1] = before[plane : plane + 1]
                u[c, 7 + plane, row : row + 1] = behind[plane : plane + 1]
            place += 2
    roll_field(u, ur, (7, 8))
    for x in range(4):
        total = side_part(x, u, ur, s, sr, d)
        scale = bond_scale * s[x + 3, LOW : LOW + 8]
        for c in range(3):
            velocity = v_in[c, x] + time_step * (scale * (force[c, x] + total[c]))
            v_out[c, x] = velocity
            u_out[c, x] = near[c, x] + time_step * velocity


def f32(*shape):
    return jax.ShapeDtypeStruct(shape, jnp.float32)


def arrays(*tail):
    shapes = [f32(3, *tail), f32(3, 4, *tail), f32(*tail), f32(4, *tail)]
    return shapes + [jax.ShapeDtypeStruct((6,) + tail, jnp.int32)]


LAYERS = arrays(PLANES, ROWS, 128)
FLAT = arrays(PLANES * ROWS, 128)
LINES = arrays(6, 16, 128) + [jax.ShapeDtypeStruct((6, 4, 6, 16, 128), jnp.int32)]


def scratch(shapes):
    return [pltpu.VMEM(s.shape, s.dtype) for s in shapes]


def call(kernel, outputs, buffers, *operands, flops=1000):
    return pl.pallas_call(
        kernel,
        out_shape=outputs,
        in_specs=[pl.BlockSpec(memory_space=pltpu.VMEM)] * len(operands),
        out_specs=[pl.BlockSpec(memory_space=pltpu.VMEM)] * len(outputs),
        scratch_shapes=scratch(buffers),
        compiler_params=pltpu.CompilerParams(vmem_limit_bytes=32 * 1024 * 1024),
        cost_estimate=pl.CostEstimate(flops=flops, bytes_accessed=flops, transcendentals=0),
    )(*operands)


def swapped(value, axis, first):
    pairs = [(i, i + 1) for i in range(first, lax.axis_size(axis) - 1, 2)]
    return lax.ppermute(value, axis, pairs + [(j, i) for i, j in pairs])


def shards(displacement, velocity, stiffness, damage):
    point = f32(3, 4, 8, 128)
    edge = f32(3, 6, 8, 128)
    fields = joined_fields(displacement, velocity, stiffness, damage)
    far_x, near_x = call(pack_x, [f32(21, 8, 128)] * 2, [], fields)
    far_x = swapped(far_x, "gx", 1)
    near_x = swapped(near_x, "gx", 0)
    (force,) = call(first_own, [point], LAYERS, fields, flops=4_000_000)
    message = f32(Y_ROWS, 128)
    b, a, v_part = call(
        first_sides, [message, message, point], FLAT + [FLAT[0], message, message], fields, far_x, near_x, force
    )
    b = swapped(b, "gy", 1)
    a = swapped(a, "gy", 0)
    lines = call(second_own, LINES, [FLAT[0], FLAT[2], FLAT[4]], fields, far_x, near_x, flops=2_000_000)
    velocity, near, edge, far_u, near_u = call(
        second_rows,
        [point, point, edge, f32(96, 128), f32(96, 128)],
        LINES + [f32(3, 64, 128)],
        fields,
        b,
        a,
        v_part,
        *lines,
    )
    kept = (fields, far_x, near_x, b, a, near, edge)
    far_u = swapped(far_u.reshape(12, 8, 128), "gx", 1).reshape(96, 128)
    near_u = swapped(near_u.reshape(12, 8, 128), "gx", 0).reshape(96, 128)
    force, *stiff = call(last_own, [point] + LAYERS[2:], LAYERS[:2], *kept, flops=4_000_000)
    return tuple(
        call(last_sides, [point, point], LAYERS[:2], near, velocity, force, *stiff, far_u, near_u)
    )


def solution(mesh):
    return jax.shard_map(
        shards,
        mesh=mesh,
        in_specs=(
            P(None, "gx", "gy", None),
            P(None, "gx", "gy", None),
            P("gx", "gy", None),
            P(None, "gx", "gy", None),
        ),
        out_specs=(P(None, "gx", "gy", None), P(None, "gx", "gy", None)),
        check_vma=False,
    )
```

```python
import math

import jax
import jax.numpy as jnp
from jax import lax
from jax.experimental import pallas as pl
from jax.experimental.pallas import tpu as pltpu
from jax.sharding import PartitionSpec as P

STEPS = 2

time_step = 0.02
bond_scale = 100.0

PLANES, ROWS = 10, 16
LOW = 3
V, K, D, FIELD_COUNT = 3, 6, 7, 13
ROLLS = (-2, -1, 1, 2)


def bond_offsets():
    table = []
    for step_x in range(0, 4):
        for step_y in range(-3, 4):
            for step_z in range(-3, 4):
                if step_x * step_x + step_y * step_y + step_z * step_z <= 9 and (
                    step_x,
                    step_y,
                    step_z,
                ) > (0, 0, 0):
                    table.append((step_x, step_y, step_z))
    return table


BONDS = list(enumerate(bond_offsets()))

RIGHT_WORDS = [(3, 2, w) for w in range(1, 6)] + [(2, 1, w) for w in range(3, 6)] + [(1, 0, 5)]


def y_slots(upward):
    slots = []
    place = 0

    def put(kind, comp, depth, plane, count):
        nonlocal place
        here = LOW + 7 - depth if upward else LOW + depth
        there = LOW - 1 - depth if upward else LOW + 8 + depth
        slots.append((kind, comp, here, there, plane, count, place))
        place += count

    for kind, comps in (("u", 3), ("s", 1)):
        for comp in range(comps):
            for depth in range(3):
                put(kind, comp, depth, *((1, 8) if depth < 2 else (3, 4)))
    for comp in range(3):
        for depth in range(3):
            put("d", comp, depth, 3, 4)
    words = ((0, 1, 2, 3, 4, 5), (0, 1, 3, 5), (1,)) if upward else ((1, 2, 3, 4), (1, 3))
    for depth, row_words in enumerate(words):
        for word in row_words:
            put("w", word, depth, *((3, 4) if upward and word < 2 else (1, 6)))
    return slots, place


UP_SLOTS, UP_ROWS = y_slots(True)
DOWN_SLOTS, DOWN_ROWS = y_slots(False)
Y_ROWS = -(-max(UP_ROWS, DOWN_ROWS) // 8) * 8

CORNER_ROWS = (1, 2, 11, 12)


def line_of(row):
    return {0: 0, 1: 1, 2: 2, 11: 3, 12: 4, 13: 5, 3: 0, 4: 1, 5: 2, 8: 3, 9: 4, 10: 5}[row]


def spot(ref, plane, row, count=8):
    if ref.shape[-2] == ROWS:
        return (plane, slice(row, row + count))
    return (slice(plane * ROWS + row, plane * ROWS + row + count),)


def rolled(value, distance):
    return pltpu.roll(value, (-distance) % 128, value.ndim - 1)


def lane_mask(distance):
    lane = lax.broadcasted_iota(jnp.int32, (8, 128), 1)
    return lane < 128 - distance if distance > 0 else lane >= -distance


def roll_field(source, target, planes, halves=(0, 8)):
    for c in range(3):
        for plane in planes:
            for half in halves:
                value = source[(c,) + spot(source, plane, half)]
                for i, ez in enumerate(ROLLS):
                    target[(c, i) + spot(target, plane, half)] = rolled(value, ez)


def roll_stiffness(source, target, planes, halves=(0, 8)):
    for plane in planes:
        for half in halves:
            value = source[spot(source, plane, half)]
            for i, ez in enumerate(ROLLS):
                moved = jnp.where(lane_mask(ez), rolled(value, ez), 0.0)
                target[(i,) + spot(target, plane, half)] = moved


def add_bond(total, source, target, length, weight):
    sep = [a - b for a, b in zip(source, target)]
    square = sep[0] * sep[0] + sep[1] * sep[1] + sep[2] * sep[2]
    factor = (1.0 / length - lax.rsqrt(square)) * weight
    return [t + factor * p for t, p in zip(total, sep)]


def intact(q, words, value):
    return jnp.where(jnp.bitwise_and(words, 1 << (q % 11)) == 0, value, 0.0)


def rolled_back(part, ez):
    mask = lane_mask(-ez)
    return [jnp.where(mask, rolled(p, -ez), 0.0) for p in part]


def accumulate(plane, base, owned, reacted, u, ur, s, sr, d):
    here = [u[(c,) + spot(u, plane, base)] for c in range(3)]
    total = [jnp.zeros((8, 128), jnp.float32) for _ in range(3)]

    for ez in range(-3, 4):
        for q, (ex, ey, _) in [b for b in owned if b[1][2] == ez]:
            row, at = base + ey, plane + ex
            length = math.sqrt(ex * ex + ey * ey + ez * ez)
            if ez == 0:
                source = [u[(c,) + spot(u, at, row)] for c in range(3)]
                stiff = s[spot(s, at, row)]
            elif abs(ez) < 3:
                i = ROLLS.index(ez)
                source = [ur[(c, i) + spot(ur, at, row)] for c in range(3)]
                stiff = sr[(i,) + spot(sr, at, row)]
            else:
                source = [rolled(h, ez) for h in here]
                stiff = jnp.where(lane_mask(ez), rolled(s[spot(s, at, row)], ez), 0.0)
            target = [h - float(e) for h, e in zip(here, (ex, ey, ez))]
            words = d[(q // 11,) + spot(d, plane, base)]
            total = add_bond(total, source, target, length, intact(q, words, stiff))
        bonds = [b for b in reacted if b[1][2] == ez]
        if not bonds:
            continue
        moved = here if ez == 0 else [rolled(h, ez) for h in here]
        part = total if ez == 0 else [jnp.zeros((8, 128), jnp.float32) for _ in range(3)]
        for q, (ex, ey, _) in bonds:
            row, at = base - ey, plane - ex
            length = math.sqrt(ex * ex + ey * ey + ez * ez)
            source = [u[(c,) + spot(u, at, row)] for c in range(3)]
            target = [h + float(e) for h, e in zip(moved, (ex, ey, ez))]
            stiff = s[spot(s, at, row)]
            words = d[(q // 11,) + spot(d, at, row)]
            part = add_bond(part, source, target, length, intact(q, words, stiff))
        if ez == 0:
            total = part
        else:
            total = [t + p for t, p in zip(total, rolled_back(part, ez))]
    return total


def accumulate_row(row, sources, u, d, other):
    ou, our, os, osr, od, odr = other

    def line(plain, turned, lead, ez, plane, at):
        ref, lead = (plain, lead) if ez == 0 else (turned, lead + (ROLLS.index(ez),))
        return ref[lead + (line_of(at), slice(plane, plane + 8))]

    here = [u[c, line_of(row), 2:10] for c in range(3)]
    total = [jnp.zeros((8, 128), jnp.float32) for _ in range(3)]
    for q, bond in BONDS:
        length = math.sqrt(sum(e * e for e in bond))
        for sign in (1, -1):
            ex, ey, ez = (sign * e for e in bond)
            if row + ey not in sources:
                continue
            plane, at = 2 + ex, row + ey
            source = [line(ou, our, (c,), ez, plane, at) for c in range(3)]
            stiff = line(os, osr, (), ez, plane, at)
            if sign > 0:
                word = d[q // 11, line_of(row), 2:10]
            else:
                word = line(od, odr, (q // 11,), ez, plane, at)
            target = [h - float(e) for h, e in zip(here, (ex, ey, ez))]
            total = add_bond(total, source, target, length, intact(q, word, stiff))
    return [part[0:4] for part in total]


def put_own(fields, u, s, d):
    for x in range(4):
        if u is not None:
            for c in range(3):
                u[(c,) + spot(u, x + 3, LOW)] = fields[c, x]
        if s is not None:
            s[spot(s, x + 3, LOW)] = jnp.sqrt(fields[K, x])
        for w in range(6):
            d[(w,) + spot(d, x + 3, LOW)] = fields[D + w, x].astype(jnp.int32)


def put_zeros(ref, leads, planes, row, count):
    for lead in leads:
        for plane in planes:
            ref[lead + spot(ref, plane, row, count)] = jnp.zeros((count, 128), ref.dtype)


def put_sides(even, near, far, u, s, d):
    rows = slice(LOW, LOW + 8)

    def left(i):
        return jnp.where(even, far[i], near[i])

    def right(i):
        return jnp.where(even, near[i], far[i])

    for plane in range(3):
        for c in range(3):
            if u is not None:
                u[(c,) + spot(u, plane, LOW)] = left(3 * c + plane)
                u[(c,) + spot(u, 7 + plane, LOW)] = right(3 * c + plane)
        s[spot(s, plane, LOW)] = jnp.sqrt(left(9 + plane))
        s[spot(s, 7 + plane, LOW)] = jnp.sqrt(right(9 + plane))
    for i, (_, plane, word) in enumerate(RIGHT_WORDS):
        d[(word,) + spot(d, plane, LOW)] = left(12 + i).astype(jnp.int32)


def message_lines(even, a, b):
    for slots, above in ((DOWN_SLOTS, True), (UP_SLOTS, False)):
        for slot in slots:
            place, count = slot[6], slot[5]
            one, two = a[place : place + count], b[place : place + count]
            yield slot, jnp.where(even, one, two) if above else jnp.where(even, two, one)


def put_lines(even, a, b, u, s, d, edge):
    for (kind, comp, _, there, plane, count, _), value in message_lines(even, a, b):
        at, planes = line_of(there), slice(plane - 1, plane - 1 + count)
        if kind == "u":
            u[comp, at, planes] = value
        elif kind == "s":
            s[at, planes] = value
        elif kind == "d":
            edge[comp, at, 0:4] = value
        else:
            d[comp, at, planes] = value.astype(jnp.int32)


def put_rows(even, a, b, s, d, wanted):
    for (kind, comp, _, there, plane, count, _), value in message_lines(even, a, b):
        for i in range(count):
            if (plane + i in wanted) and kind == "s":
                s[spot(s, plane + i, there, 1)] = value[i : i + 1]
            elif (plane + i in wanted) and kind == "w":
                d[(comp,) + spot(d, plane + i, there, 1)] = value[i : i + 1].astype(jnp.int32)


def even_place():
    return tuple(lax.axis_index(axis) % 2 == 0 for axis in ("gx", "gy"))


def joined_fields(displacement, velocity, stiffness, damage):
    parts = (displacement, velocity, stiffness[None], damage)
    total, before = 0.0, 0
    for part in parts:
        count = part.shape[0]
        widths = ((before, FIELD_COUNT - before - count, 0),) + ((0, 0, 0),) * 3
        total = total + lax.pad(part, part.dtype.type(0), widths).astype(jnp.float32)
        before += count
    return total


def pack_x(fields, far, near):
    even, _ = even_place()
    for i, field in enumerate((0, 1, 2, K)):
        for plane in range(3):
            one, two = fields[field, plane + 1], fields[field, plane]
            near[3 * i + plane] = jnp.where(even, one, two)
            far[3 * i + plane] = jnp.where(even, two, one)
    for i, (plane, _, word) in enumerate(RIGHT_WORDS):
        near[12 + i] = fields[D + word, plane]
        far[12 + i] = fields[D + word, plane]


SIDES = (0, 1, 2, 7, 8, 9)
OUTER = ((0, LOW), (LOW + 8, ROWS - LOW - 8))
EACH = ((0,), (1,), (2,))


def own_part(u, ur, s, sr, d, force):
    roll_field(u, ur, range(3, 7))
    roll_stiffness(s, sr, range(3, 7))
    for i in range(4):
        for plane in (7, 8):
            put_zeros(ur, [(c, i) for c in range(3)], (plane,), 0, ROWS)
            put_zeros(sr, [(i,)], (plane,), 0, ROWS)

    @pl.loop(0, 4)
    def _(x):
        total = accumulate(x + 3, LOW, BONDS, BONDS, u, ur, s, sr, d)
        for c in range(3):
            force[c, x] = total[c]


def side_part(x, u, ur, s, sr, d):
    owned = [b for b in BONDS if x + b[1][0] > 3]
    reacted = [b for b in BONDS if x - b[1][0] < 0]
    return accumulate(x + 3, LOW, owned, reacted, u, ur, s, sr, d)


def first_own(fields, force, u, ur, s, sr, d):
    put_zeros(u, EACH, SIDES, 0, ROWS)
    put_zeros(s, [()], SIDES, 0, ROWS)
    for row, count in OUTER:
        put_zeros(u, EACH, range(3, 7), row, count)
        put_zeros(s, [()], range(3, 7), row, count)
        put_zeros(d, [(w,) for w in range(6)], range(3, 7), row, count)
    put_own(fields, u, s, d)
    own_part(u, ur, s, sr, d, force)


def first_sides(fields, far_x, near_x, force, b, a, v_part, u, ur, s, sr, d, near, up, down):
    even_x, even = even_place()
    for row, count in OUTER:
        put_zeros(u, EACH, SIDES, row, count)
        put_zeros(s, [()], SIDES, row, count)
    put_own(fields, u, s, d)
    put_sides(even_x, near_x, far_x, u, s, d)
    roll_field(u, ur, (7, 8))
    roll_stiffness(s, sr, (7, 8))
    for x in range(4):
        total = side_part(x, u, ur, s, sr, d)
        scale = bond_scale * s[spot(s, x + 3, LOW)]
        for c in range(3):
            velocity = fields[V + c, x] + time_step * (scale * (force[c, x] + total[c]))
            v_part[c, x] = velocity
            near[(c,) + spot(u, x + 3, LOW)] = fields[c, x] + time_step * velocity

    for slots, message in ((UP_SLOTS, up), (DOWN_SLOTS, down)):
        for kind, comp, here, _, plane, count, place in slots:
            lines = pl.ds(plane * ROWS + here, count, stride=ROWS)
            if kind == "u":
                value = u[comp, lines]
            elif kind == "s":
                value = s[lines]
            elif kind == "d":
                value = near[comp, lines]
            else:
                value = d[comp, lines].astype(jnp.float32)
            message[place : place + count] = value
    a[...] = jnp.where(even, up[...], down[...])
    b[...] = jnp.where(even, down[...], up[...])


def roll_lines(u, ur, s, sr, d, dr, words):
    for at in range(6):
        for i, ez in enumerate(ROLLS):
            for w in words[at]:
                dr[w, i, at, 0:8] = rolled(d[w, at, 0:8], ez)
            for c in range(3):
                ur[c, i, at, 0:8] = rolled(u[c, at, 0:8], ez)
            sr[i, at, 0:8] = jnp.where(lane_mask(ez), rolled(s[at, 0:8], ez), 0.0)


def second_own(fields, far_x, near_x, u, ur, s, sr, d, dr, whole_u, whole_s, whole_d):
    even_x, _ = even_place()
    put_own(fields, whole_u, whole_s, whole_d)
    put_sides(even_x, near_x, far_x, whole_u, whole_s, whole_d)
    for row in (3, 4, 5, 8, 9, 10):
        at, lines = line_of(row), pl.ds(ROWS + row, 8, stride=ROWS)
        for c in range(3):
            u[c, at, 0:8] = whole_u[c, lines]
        s[at, 0:8] = whole_s[lines]
        for w in range(6):
            d[w, at, 0:8] = whole_d[w, lines]
    roll_lines(u, ur, s, sr, d, dr, [range(6)] * 6)


def second_rows(fields, b, a, v_part, u, ur, s, sr, d, dr, v_out, near, edge, to_far, to_near, hu, hur, hs, hsr, hd, hdr, sums):
    even_x, even = even_place()
    put_lines(even, a, b, hu, hs, hd, edge)
    sent = UP_SLOTS + DOWN_SLOTS
    words = [[k[1] for k in sent if k[0] == "w" and line_of(k[3]) == at] for at in range(6)]
    roll_lines(hu, hur, hs, hsr, hd, hdr, words)
    beside = (u, ur, s, sr, d, dr)
    beyond = (hu, hur, hs, hsr, hd, hdr)
    for row in (3, 4, 5, 8, 9, 10):
        sources = range(0, LOW) if row < LOW + 4 else range(LOW + 8, LOW + 11)
        force = accumulate_row(row, sources, u, d, beyond)
        for c in range(3):
            sums[c, 8 * (row - LOW) : 8 * (row - LOW) + 4] = force[c]
    for c in range(3):
        for row in (6, 7):
            sums[c, 8 * (row - LOW) : 8 * (row - LOW) + 8] = jnp.zeros((8, 128), jnp.float32)
    for row in (0, 1, 2, 11, 12, 13):
        sources = range(LOW, LOW + 3) if row < LOW + 4 else range(LOW + 5, LOW + 8)
        force = accumulate_row(row, sources, hu, hd, beside)
        at = line_of(row)
        scale = (time_step * time_step * bond_scale) * hs[at, 2:6]
        for c in range(3):
            edge[c, at, 0:4] += scale * force[c]
    for x in range(4):
        scale = (time_step * bond_scale) * jnp.sqrt(fields[K, x])
        for c in range(3):
            velocity = v_part[c, x] + scale * sums[c, pl.ds(x, 8, stride=8)]
            v_out[c, x] = velocity
            near[c, x] = fields[c, x] + time_step * velocity

    place = 0
    for c in range(3):
        for plane in range(3):
            one, two = near[c, plane + 1], near[c, plane]
            to_near[place : place + 8] = jnp.where(even_x, one, two)
            to_far[place : place + 8] = jnp.where(even_x, two, one)
            place += 8
    for c in range(3):
        for row in CORNER_ROWS:
            one, two = edge[c, line_of(row), 2:4], edge[c, line_of(row), 0:2]
            to_near[place : place + 2] = jnp.where(even_x, one, two)
            to_far[place : place + 2] = jnp.where(even_x, two, one)
            place += 2


def last_own(fields, far_x, near_x, b, a, near, edge, force, s, sr, d, u, ur):
    even_x, even = even_place()
    put_zeros(u, EACH, SIDES, 0, ROWS)
    put_zeros(s, [()], SIDES, 0, ROWS)
    put_own(fields, None, s, d)
    put_rows(even, a, b, s, d, range(3, 7))
    for c in range(3):
        u[c, 3:7, LOW : LOW + 8] = near[c]
        for row in (0, 1, 2, 11, 12, 13):
            for x in range(4):
                u[c, x + 3, row : row + 1] = edge[c, line_of(row), x : x + 1]
    own_part(u, ur, s, sr, d, force)
    put_sides(even_x, near_x, far_x, None, s, d)
    put_rows(even, a, b, s, d, SIDES)
    roll_stiffness(s, sr, (7, 8))


def last_sides(near, v_in, force, s, sr, d, far_u, near_u, u_out, v_out, u, ur, ready, sems):
    even_x, _ = even_place()
    for c in range(3):
        u[c, 3:7, LOW : LOW + 8] = near[c]
    put_zeros(u, EACH, SIDES, 0, LOW)
    put_zeros(u, EACH, SIDES, LOW + 8, ROWS - LOW - 8)
    place = 0
    for c in range(3):
        for plane in range(3):
            one, two = near_u[place : place + 8], far_u[place : place + 8]
            u[c, plane, LOW : LOW + 8] = jnp.where(even_x, two, one)
            u[c, 7 + plane, LOW : LOW + 8] = jnp.where(even_x, one, two)
            place += 8
    for c in range(3):
        for row in CORNER_ROWS:
            one, two = near_u[place : place + 2], far_u[place : place + 2]
            before, behind = jnp.where(even_x, two, one), jnp.where(even_x, one, two)
            for plane in range(2):
                u[c, 1 + plane, row : row + 1] = before[plane : plane + 1]
                u[c, 7 + plane, row : row + 1] = behind[plane : plane + 1]
            place += 2
    roll_field(u, ur, (7, 8))
    copies = []
    for x in range(4):
        total = side_part(x, u, ur, s, sr, d)
        scale = bond_scale * s[x + 3, LOW : LOW + 8]
        for c in range(3):
            velocity = v_in[c, x] + time_step * (scale * (force[c, x] + total[c]))
            ready[1, c, x] = velocity
            ready[0, c, x] = near[c, x] + time_step * velocity
        for i, out in enumerate((u_out, v_out)):
            copy = pltpu.make_async_copy(ready.at[i, :, x], out.at[:, x], sems.at[i, x])
            copy.start()
            copies.append(copy)
    for copy in copies:
        copy.wait()


def f32(*shape):
    return jax.ShapeDtypeStruct(shape, jnp.float32)


def arrays(*tail):
    shapes = [f32(3, *tail), f32(3, 4, *tail), f32(*tail), f32(4, *tail)]
    return shapes + [jax.ShapeDtypeStruct((6,) + tail, jnp.int32)]


LAYERS = arrays(PLANES, ROWS, 128)
FLAT = arrays(PLANES * ROWS, 128)
LINES = arrays(6, 16, 128) + [jax.ShapeDtypeStruct((6, 4, 6, 16, 128), jnp.int32)]


def scratch(shapes):
    return [pltpu.VMEM(s.shape, s.dtype) for s in shapes]


def call(kernel, outputs, buffers, *operands, flops=1000, space=pltpu.VMEM, extra=()):
    return pl.pallas_call(
        kernel,
        out_shape=outputs,
        in_specs=[pl.BlockSpec(memory_space=pltpu.VMEM)] * len(operands),
        out_specs=[pl.BlockSpec(memory_space=space)] * len(outputs),
        scratch_shapes=scratch(buffers) + list(extra),
        compiler_params=pltpu.CompilerParams(vmem_limit_bytes=32 * 1024 * 1024),
        cost_estimate=pl.CostEstimate(flops=flops, bytes_accessed=flops, transcendentals=0),
    )(*operands)


def swapped(value, axis, first):
    pairs = [(i, i + 1) for i in range(first, lax.axis_size(axis) - 1, 2)]
    return lax.ppermute(value, axis, pairs + [(j, i) for i, j in pairs])


def shards(displacement, velocity, stiffness, damage):
    point = f32(3, 4, 8, 128)
    edge = f32(3, 6, 8, 128)
    fields = joined_fields(displacement, velocity, stiffness, damage)
    far_x, near_x = call(pack_x, [f32(21, 8, 128)] * 2, [], fields)
    far_x = swapped(far_x, "gx", 1)
    near_x = swapped(near_x, "gx", 0)
    (force,) = call(first_own, [point], LAYERS, fields, flops=4_000_000)
    message = f32(Y_ROWS, 128)
    b, a, v_part = call(
        first_sides, [message, message, point], FLAT + [FLAT[0], message, message], fields, far_x, near_x, force
    )
    b = swapped(b, "gy", 1)
    a = swapped(a, "gy", 0)
    lines = call(second_own, LINES, [FLAT[0], FLAT[2], FLAT[4]], fields, far_x, near_x, flops=2_000_000)
    velocity, near, edge, far_u, near_u = call(
        second_rows,
        [point, point, edge, f32(96, 128), f32(96, 128)],
        LINES + [f32(3, 64, 128)],
        fields,
        b,
        a,
        v_part,
        *lines,
    )
    kept = (fields, far_x, near_x, b, a, near, edge)
    far_u = swapped(far_u.reshape(12, 8, 128), "gx", 1).reshape(96, 128)
    near_u = swapped(near_u.reshape(12, 8, 128), "gx", 0).reshape(96, 128)
    force, *stiff = call(last_own, [point] + LAYERS[2:], LAYERS[:2], *kept, flops=4_000_000)
    return tuple(
        call(
            last_sides,
            [point, point],
            LAYERS[:2] + [f32(2, 3, 4, 8, 128)],
            near,
            velocity,
            force,
            *stiff,
            far_u,
            near_u,
            space=pl.ANY,
            extra=[pltpu.SemaphoreType.DMA((2, 4))],
        )
    )


def solution(mesh):
    return jax.shard_map(
        shards,
        mesh=mesh,
        in_specs=(
            P(None, "gx", "gy", None),
            P(None, "gx", "gy", None),
            P("gx", "gy", None),
            P(None, "gx", "gy", None),
        ),
        out_specs=(P(None, "gx", "gy", None), P(None, "gx", "gy", None)),
        check_vma=False,
    )
```

```python
import math

import jax
import jax.numpy as jnp
from jax import lax
from jax.experimental import pallas as pl
from jax.experimental.pallas import tpu as pltpu
from jax.sharding import PartitionSpec as P

STEPS = 2

time_step = 0.02
bond_scale = 100.0

PLANES, ROWS = 10, 16
LOW = 3
V, K, D, FIELD_COUNT = 3, 6, 7, 13
ROLLS = (-2, -1, 1, 2)


def bond_offsets():
    table = []
    for step_x in range(0, 4):
        for step_y in range(-3, 4):
            for step_z in range(-3, 4):
                if step_x * step_x + step_y * step_y + step_z * step_z <= 9 and (
                    step_x,
                    step_y,
                    step_z,
                ) > (0, 0, 0):
                    table.append((step_x, step_y, step_z))
    return table


BONDS = list(enumerate(bond_offsets()))

RIGHT_WORDS = [(3, 2, w) for w in range(1, 6)] + [(2, 1, w) for w in range(3, 6)]
X_TILES = 12 + len(RIGHT_WORDS)


def y_slots(upward):
    slots = []
    place = 0

    def put(kind, comp, depth, plane, count):
        nonlocal place
        here = LOW + 7 - depth if upward else LOW + depth
        there = LOW - 1 - depth if upward else LOW + 8 + depth
        slots.append((kind, comp, here, there, plane, count, place))
        place += count

    for kind, comps in (("u", 3), ("s", 1)):
        for comp in range(comps):
            for depth in range(3):
                put(kind, comp, depth, *((1, 8) if depth < 2 else (3, 4)))
    for comp in range(3):
        for depth in range(3):
            put("d", comp, depth, 3, 4)
    words = ((0, 1, 2, 3, 4, 5), (0, 1, 3, 5), (1,)) if upward else ((1, 2, 3, 4), (1, 3))
    for depth, row_words in enumerate(words):
        for word in row_words:
            put("w", word, depth, *((3, 4) if upward and word < 2 else (1, 6)))
    return slots, place


UP_SLOTS, UP_ROWS = y_slots(True)
DOWN_SLOTS, DOWN_ROWS = y_slots(False)
Y_ROWS = -(-max(UP_ROWS, DOWN_ROWS) // 8) * 8

CORNER_ROWS = (1, 2, 11, 12)


def line_of(row):
    return {0: 0, 1: 1, 2: 2, 11: 3, 12: 4, 13: 5, 3: 0, 4: 1, 5: 2, 8: 3, 9: 4, 10: 5}[row]


def spot(ref, plane, row, count=8):
    if ref.shape[-2] == ROWS:
        return (plane, slice(row, row + count))
    return (slice(plane * ROWS + row, plane * ROWS + row + count),)


def rolled(value, distance):
    return pltpu.roll(value, (-distance) % 128, value.ndim - 1)


def lane_mask(distance):
    lane = lax.broadcasted_iota(jnp.int32, (8, 128), 1)
    return lane < 128 - distance if distance > 0 else lane >= -distance


def roll_field(source, target, planes, halves=(0, 8)):
    for c in range(3):
        for plane in planes:
            for half in halves:
                value = source[(c,) + spot(source, plane, half)]
                for i, ez in enumerate(ROLLS):
                    target[(c, i) + spot(target, plane, half)] = rolled(value, ez)


def roll_stiffness(source, target, planes, halves=(0, 8)):
    for plane in planes:
        for half in halves:
            value = source[spot(source, plane, half)]
            for i, ez in enumerate(ROLLS):
                moved = jnp.where(lane_mask(ez), rolled(value, ez), 0.0)
                target[(i,) + spot(target, plane, half)] = moved


def add_bond(total, source, target, length, weight):
    sep = [a - b for a, b in zip(source, target)]
    square = sep[0] * sep[0] + sep[1] * sep[1] + sep[2] * sep[2]
    factor = (1.0 / length - lax.rsqrt(square)) * weight
    return [t + factor * p for t, p in zip(total, sep)]


def intact(q, words, value):
    return jnp.where(jnp.bitwise_and(words, 1 << (q % 11)) == 0, value, 0.0)


def rolled_back(part, ez):
    mask = lane_mask(-ez)
    return [jnp.where(mask, rolled(p, -ez), 0.0) for p in part]


def accumulate(plane, base, owned, reacted, u, ur, s, sr, d):
    here = [u[(c,) + spot(u, plane, base)] for c in range(3)]
    total = [jnp.zeros((8, 128), jnp.float32) for _ in range(3)]

    for ez in range(-3, 4):
        for q, (ex, ey, _) in [b for b in owned if b[1][2] == ez]:
            row, at = base + ey, plane + ex
            length = math.sqrt(ex * ex + ey * ey + ez * ez)
            if ez == 0:
                source = [u[(c,) + spot(u, at, row)] for c in range(3)]
                stiff = s[spot(s, at, row)]
            elif abs(ez) < 3:
                i = ROLLS.index(ez)
                source = [ur[(c, i) + spot(ur, at, row)] for c in range(3)]
                stiff = sr[(i,) + spot(sr, at, row)]
            else:
                source = [rolled(h, ez) for h in here]
                stiff = jnp.where(lane_mask(ez), rolled(s[spot(s, at, row)], ez), 0.0)
            target = [h - float(e) for h, e in zip(here, (ex, ey, ez))]
            words = d[(q // 11,) + spot(d, plane, base)]
            total = add_bond(total, source, target, length, intact(q, words, stiff))
        bonds = [b for b in reacted if b[1][2] == ez]
        if not bonds:
            continue
        moved = here if ez == 0 else [rolled(h, ez) for h in here]
        part = total if ez == 0 else [jnp.zeros((8, 128), jnp.float32) for _ in range(3)]
        for q, (ex, ey, _) in bonds:
            row, at = base - ey, plane - ex
            length = math.sqrt(ex * ex + ey * ey + ez * ez)
            source = [u[(c,) + spot(u, at, row)] for c in range(3)]
            target = [h + float(e) for h, e in zip(moved, (ex, ey, ez))]
            stiff = s[spot(s, at, row)]
            words = d[(q // 11,) + spot(d, at, row)]
            part = add_bond(part, source, target, length, intact(q, words, stiff))
        if ez == 0:
            total = part
        else:
            total = [t + p for t, p in zip(total, rolled_back(part, ez))]
    return total


def accumulate_row(row, sources, u, d, other):
    ou, our, os, osr, od, odr = other

    def line(plain, turned, lead, ez, plane, at):
        ref, lead = (plain, lead) if ez == 0 else (turned, lead + (ROLLS.index(ez),))
        return ref[lead + (line_of(at), slice(plane, plane + 8))]

    here = [u[c, line_of(row), 2:10] for c in range(3)]
    total = [jnp.zeros((8, 128), jnp.float32) for _ in range(3)]
    for q, bond in BONDS:
        length = math.sqrt(sum(e * e for e in bond))
        for sign in (1, -1):
            ex, ey, ez = (sign * e for e in bond)
            if row + ey not in sources:
                continue
            plane, at = 2 + ex, row + ey
            source = [line(ou, our, (c,), ez, plane, at) for c in range(3)]
            stiff = line(os, osr, (), ez, plane, at)
            if sign > 0:
                word = d[q // 11, line_of(row), 2:10]
            else:
                word = line(od, odr, (q // 11,), ez, plane, at)
            target = [h - float(e) for h, e in zip(here, (ex, ey, ez))]
            total = add_bond(total, source, target, length, intact(q, word, stiff))
    return [part[0:4] for part in total]


def put_own(fields, u, s, d):
    for x in range(4):
        if u is not None:
            for c in range(3):
                u[(c,) + spot(u, x + 3, LOW)] = fields[c, x]
        if s is not None:
            s[spot(s, x + 3, LOW)] = jnp.sqrt(fields[K, x])
        for w in range(6):
            d[(w,) + spot(d, x + 3, LOW)] = fields[D + w, x].astype(jnp.int32)


def put_zeros(ref, leads, planes, row, count):
    for lead in leads:
        for plane in planes:
            ref[lead + spot(ref, plane, row, count)] = jnp.zeros((count, 128), ref.dtype)


def put_sides(even, near, far, u, s, d):
    rows = slice(LOW, LOW + 8)

    def left(i):
        return jnp.where(even, far[i], near[i])

    def right(i):
        return jnp.where(even, near[i], far[i])

    for plane in range(3):
        for c in range(3):
            if u is not None:
                u[(c,) + spot(u, plane, LOW)] = left(3 * c + plane)
                u[(c,) + spot(u, 7 + plane, LOW)] = right(3 * c + plane)
        s[spot(s, plane, LOW)] = jnp.sqrt(left(9 + plane))
        s[spot(s, 7 + plane, LOW)] = jnp.sqrt(right(9 + plane))
    for i, (_, plane, word) in enumerate(RIGHT_WORDS):
        d[(word,) + spot(d, plane, LOW)] = left(12 + i).astype(jnp.int32)
    d[(5,) + spot(d, 0, LOW)] = jnp.zeros((8, 128), jnp.int32)


def message_lines(even, a, b):
    for slots, above in ((DOWN_SLOTS, True), (UP_SLOTS, False)):
        for slot in slots:
            place, count = slot[6], slot[5]
            one, two = a[place : place + count], b[place : place + count]
            yield slot, jnp.where(even, one, two) if above else jnp.where(even, two, one)


def put_lines(even, a, b, u, s, d, edge):
    for (kind, comp, _, there, plane, count, _), value in message_lines(even, a, b):
        at, planes = line_of(there), slice(plane - 1, plane - 1 + count)
        if kind == "u":
            u[comp, at, planes] = value
        elif kind == "s":
            s[at, planes] = value
        elif kind == "d":
            edge[comp, at, 0:4] = value
        else:
            d[comp, at, planes] = value.astype(jnp.int32)


def put_rows(even, a, b, s, d, wanted):
    for (kind, comp, _, there, plane, count, _), value in message_lines(even, a, b):
        for i in range(count):
            if (plane + i in wanted) and kind == "s":
                s[spot(s, plane + i, there, 1)] = value[i : i + 1]
            elif (plane + i in wanted) and kind == "w":
                d[(comp,) + spot(d, plane + i, there, 1)] = value[i : i + 1].astype(jnp.int32)


def even_place():
    return tuple(lax.axis_index(axis) % 2 == 0 for axis in ("gx", "gy"))


def joined_fields(displacement, velocity, stiffness, damage):
    parts = (displacement, velocity, stiffness[None], damage)
    total, before = 0.0, 0
    for part in parts:
        count = part.shape[0]
        widths = ((before, FIELD_COUNT - before - count, 0),) + ((0, 0, 0),) * 3
        total = total + lax.pad(part, part.dtype.type(0), widths).astype(jnp.float32)
        before += count
    return total


def pack_x(fields, far, near):
    even, _ = even_place()
    for i, field in enumerate((0, 1, 2, K)):
        for plane in range(3):
            one, two = fields[field, plane + 1], fields[field, plane]
            if field == K and plane == 0:
                ((q, _),) = [b for b in BONDS if b[1][0] == 3]
                one = intact(q, fields[D + q // 11, 1].astype(jnp.int32), one)
            near[3 * i + plane] = jnp.where(even, one, two)
            far[3 * i + plane] = jnp.where(even, two, one)
    for i, (plane, _, word) in enumerate(RIGHT_WORDS):
        near[12 + i] = fields[D + word, plane]
        far[12 + i] = fields[D + word, plane]


SIDES = (0, 1, 2, 7, 8, 9)
OUTER = ((0, LOW), (LOW + 8, ROWS - LOW - 8))
EACH = ((0,), (1,), (2,))


def own_part(u, ur, s, sr, d, force):
    roll_field(u, ur, range(3, 7))
    roll_stiffness(s, sr, range(3, 7))
    for i in range(4):
        for plane in (7, 8):
            put_zeros(ur, [(c, i) for c in range(3)], (plane,), 0, ROWS)
            put_zeros(sr, [(i,)], (plane,), 0, ROWS)

    @pl.loop(0, 4)
    def _(x):
        total = accumulate(x + 3, LOW, BONDS, BONDS, u, ur, s, sr, d)
        for c in range(3):
            force[c, x] = total[c]


def side_part(x, u, ur, s, sr, d):
    owned = [b for b in BONDS if x + b[1][0] > 3]
    reacted = [b for b in BONDS if x - b[1][0] < 0]
    return accumulate(x + 3, LOW, owned, reacted, u, ur, s, sr, d)


def first_own(fields, force, u, ur, s, sr, d):
    put_zeros(u, EACH, SIDES, 0, ROWS)
    put_zeros(s, [()], SIDES, 0, ROWS)
    for row, count in OUTER:
        put_zeros(u, EACH, range(3, 7), row, count)
        put_zeros(s, [()], range(3, 7), row, count)
        put_zeros(d, [(w,) for w in range(6)], range(3, 7), row, count)
    put_own(fields, u, s, d)
    own_part(u, ur, s, sr, d, force)


def first_sides(fields, far_x, near_x, force, b, a, v_part, u, ur, s, sr, d, near, up, down):
    even_x, even = even_place()
    for row, count in OUTER:
        put_zeros(u, EACH, SIDES, row, count)
        put_zeros(s, [()], SIDES, row, count)
    put_own(fields, u, s, d)
    put_sides(even_x, near_x, far_x, u, s, d)
    roll_field(u, ur, (7, 8))
    roll_stiffness(s, sr, (7, 8))
    for x in range(4):
        total = side_part(x, u, ur, s, sr, d)
        scale = bond_scale * s[spot(s, x + 3, LOW)]
        for c in range(3):
            velocity = fields[V + c, x] + time_step * (scale * (force[c, x] + total[c]))
            v_part[c, x] = velocity
            near[(c,) + spot(u, x + 3, LOW)] = fields[c, x] + time_step * velocity

    for slots, message in ((UP_SLOTS, up), (DOWN_SLOTS, down)):
        for kind, comp, here, _, plane, count, place in slots:
            lines = pl.ds(plane * ROWS + here, count, stride=ROWS)
            if kind == "u":
                value = u[comp, lines]
            elif kind == "s":
                value = s[lines]
            elif kind == "d":
                value = near[comp, lines]
            else:
                value = d[comp, lines].astype(jnp.float32)
            message[place : place + count] = value
    a[...] = jnp.where(even, up[...], down[...])
    b[...] = jnp.where(even, down[...], up[...])


def roll_lines(u, ur, s, sr, d, dr, words):
    for at in range(6):
        for i, ez in enumerate(ROLLS):
            for w in words[at]:
                dr[w, i, at, 0:8] = rolled(d[w, at, 0:8], ez)
            for c in range(3):
                ur[c, i, at, 0:8] = rolled(u[c, at, 0:8], ez)
            sr[i, at, 0:8] = jnp.where(lane_mask(ez), rolled(s[at, 0:8], ez), 0.0)


def second_own(fields, far_x, near_x, u, ur, s, sr, d, dr, whole_u, whole_s, whole_d):
    even_x, _ = even_place()
    put_own(fields, whole_u, whole_s, whole_d)
    put_sides(even_x, near_x, far_x, whole_u, whole_s, whole_d)
    for row in (3, 4, 5, 8, 9, 10):
        at, lines = line_of(row), pl.ds(ROWS + row, 8, stride=ROWS)
        for c in range(3):
            u[c, at, 0:8] = whole_u[c, lines]
        s[at, 0:8] = whole_s[lines]
        for w in range(6):
            d[w, at, 0:8] = whole_d[w, lines]
    roll_lines(u, ur, s, sr, d, dr, [range(6)] * 6)


def second_rows(fields, b, a, v_part, u, ur, s, sr, d, dr, v_out, near, edge, to_far, to_near, hu, hur, hs, hsr, hd, hdr, sums):
    even_x, even = even_place()
    put_lines(even, a, b, hu, hs, hd, edge)
    sent = UP_SLOTS + DOWN_SLOTS
    words = [[k[1] for k in sent if k[0] == "w" and line_of(k[3]) == at] for at in range(6)]
    roll_lines(hu, hur, hs, hsr, hd, hdr, words)
    beside = (u, ur, s, sr, d, dr)
    beyond = (hu, hur, hs, hsr, hd, hdr)
    for row in (3, 4, 5, 8, 9, 10):
        sources = range(0, LOW) if row < LOW + 4 else range(LOW + 8, LOW + 11)
        force = accumulate_row(row, sources, u, d, beyond)
        for c in range(3):
            sums[c, 8 * (row - LOW) : 8 * (row - LOW) + 4] = force[c]
    for c in range(3):
        for row in (6, 7):
            sums[c, 8 * (row - LOW) : 8 * (row - LOW) + 8] = jnp.zeros((8, 128), jnp.float32)
    for row in (0, 1, 2, 11, 12, 13):
        sources = range(LOW, LOW + 3) if row < LOW + 4 else range(LOW + 5, LOW + 8)
        force = accumulate_row(row, sources, hu, hd, beside)
        at = line_of(row)
        scale = (time_step * time_step * bond_scale) * hs[at, 2:6]
        for c in range(3):
            edge[c, at, 0:4] += scale * force[c]
    for x in range(4):
        scale = (time_step * bond_scale) * jnp.sqrt(fields[K, x])
        for c in range(3):
            velocity = v_part[c, x] + scale * sums[c, pl.ds(x, 8, stride=8)]
            v_out[c, x] = velocity
            near[c, x] = fields[c, x] + time_step * velocity

    place = 0
    for c in range(3):
        for plane in range(3):
            one, two = near[c, plane + 1], near[c, plane]
            to_near[place : place + 8] = jnp.where(even_x, one, two)
            to_far[place : place + 8] = jnp.where(even_x, two, one)
            place += 8
    for c in range(3):
        for row in CORNER_ROWS:
            one, two = edge[c, line_of(row), 2:4], edge[c, line_of(row), 0:2]
            to_near[place : place + 2] = jnp.where(even_x, one, two)
            to_far[place : place + 2] = jnp.where(even_x, two, one)
            place += 2


def last_own(fields, far_x, near_x, b, a, near, edge, force, s, sr, d, u, ur):
    even_x, even = even_place()
    put_zeros(u, EACH, SIDES, 0, ROWS)
    put_zeros(s, [()], SIDES, 0, ROWS)
    put_own(fields, None, s, d)
    put_rows(even, a, b, s, d, range(3, 7))
    for c in range(3):
        u[c, 3:7, LOW : LOW + 8] = near[c]
        for row in (0, 1, 2, 11, 12, 13):
            for x in range(4):
                u[c, x + 3, row : row + 1] = edge[c, line_of(row), x : x + 1]
    own_part(u, ur, s, sr, d, force)
    put_sides(even_x, near_x, far_x, None, s, d)
    put_rows(even, a, b, s, d, SIDES)
    roll_stiffness(s, sr, (7, 8))


def last_sides(near, v_in, force, s, sr, d, far_u, near_u, u_out, v_out, u, ur):
    even_x, _ = even_place()
    for c in range(3):
        u[c, 3:7, LOW : LOW + 8] = near[c]
    put_zeros(u, EACH, SIDES, 0, LOW)
    put_zeros(u, EACH, SIDES, LOW + 8, ROWS - LOW - 8)
    place = 0
    for c in range(3):
        for plane in range(3):
            one, two = near_u[place : place + 8], far_u[place : place + 8]
            u[c, plane, LOW : LOW + 8] = jnp.where(even_x, two, one)
            u[c, 7 + plane, LOW : LOW + 8] = jnp.where(even_x, one, two)
            place += 8
    for c in range(3):
        for row in CORNER_ROWS:
            one, two = near_u[place : place + 2], far_u[place : place + 2]
            before, behind = jnp.where(even_x, two, one), jnp.where(even_x, one, two)
            for plane in range(2):
                u[c, 1 + plane, row : row + 1] = before[plane : plane + 1]
                u[c, 7 + plane, row : row + 1] = behind[plane : plane + 1]
            place += 2
    roll_field(u, ur, (7, 8))
    for x in range(4):
        total = side_part(x, u, ur, s, sr, d)
        scale = bond_scale * s[x + 3, LOW : LOW + 8]
        for c in range(3):
            velocity = v_in[c, x] + time_step * (scale * (force[c, x] + total[c]))
            v_out[c, x] = velocity
            u_out[c, x] = near[c, x] + time_step * velocity


def f32(*shape):
    return jax.ShapeDtypeStruct(shape, jnp.float32)


def arrays(*tail):
    shapes = [f32(3, *tail), f32(3, 4, *tail), f32(*tail), f32(4, *tail)]
    return shapes + [jax.ShapeDtypeStruct((6,) + tail, jnp.int32)]


LAYERS = arrays(PLANES, ROWS, 128)
FLAT = arrays(PLANES * ROWS, 128)
LINES = arrays(6, 16, 128) + [jax.ShapeDtypeStruct((6, 4, 6, 16, 128), jnp.int32)]


def scratch(shapes):
    return [pltpu.VMEM(s.shape, s.dtype) for s in shapes]


def call(kernel, outputs, buffers, *operands, flops=1000):
    return pl.pallas_call(
        kernel,
        out_shape=outputs,
        in_specs=[pl.BlockSpec(memory_space=pltpu.VMEM)] * len(operands),
        out_specs=[pl.BlockSpec(memory_space=pltpu.VMEM)] * len(outputs),
        scratch_shapes=scratch(buffers),
        compiler_params=pltpu.CompilerParams(vmem_limit_bytes=32 * 1024 * 1024),
        cost_estimate=pl.CostEstimate(flops=flops, bytes_accessed=flops, transcendentals=0),
    )(*operands)


def swapped(value, axis, first):
    pairs = [(i, i + 1) for i in range(first, lax.axis_size(axis) - 1, 2)]
    return lax.ppermute(value, axis, pairs + [(j, i) for i, j in pairs])


def shards(displacement, velocity, stiffness, damage):
    point = f32(3, 4, 8, 128)
    edge = f32(3, 6, 8, 128)
    fields = joined_fields(displacement, velocity, stiffness, damage)
    far_x, near_x = call(pack_x, [f32(X_TILES, 8, 128)] * 2, [], fields)
    far_x = swapped(far_x, "gx", 1)
    near_x = swapped(near_x, "gx", 0)
    (force,) = call(first_own, [point], LAYERS, fields, flops=4_000_000)
    message = f32(Y_ROWS, 128)
    b, a, v_part = call(
        first_sides, [message, message, point], FLAT + [FLAT[0], message, message], fields, far_x, near_x, force
    )
    b = swapped(b, "gy", 1)
    a = swapped(a, "gy", 0)
    lines = call(second_own, LINES, [FLAT[0], FLAT[2], FLAT[4]], fields, far_x, near_x, flops=2_000_000)
    velocity, near, edge, far_u, near_u = call(
        second_rows,
        [point, point, edge, f32(96, 128), f32(96, 128)],
        LINES + [f32(3, 64, 128)],
        fields,
        b,
        a,
        v_part,
        *lines,
    )
    kept = (fields, far_x, near_x, b, a, near, edge)
    far_u = swapped(far_u.reshape(12, 8, 128), "gx", 1).reshape(96, 128)
    near_u = swapped(near_u.reshape(12, 8, 128), "gx", 0).reshape(96, 128)
    force, *stiff = call(last_own, [point] + LAYERS[2:], LAYERS[:2], *kept, flops=4_000_000)
    return tuple(
        call(last_sides, [point, point], LAYERS[:2], near, velocity, force, *stiff, far_u, near_u)
    )


def solution(mesh):
    return jax.shard_map(
        shards,
        mesh=mesh,
        in_specs=(
            P(None, "gx", "gy", None),
            P(None, "gx", "gy", None),
            P("gx", "gy", None),
            P(None, "gx", "gy", None),
        ),
        out_specs=(P(None, "gx", "gy", None), P(None, "gx", "gy", None)),
        check_vma=False,
    )
```

```python
import math

import jax
import jax.numpy as jnp
from jax import lax
from jax.experimental import pallas as pl
from jax.experimental.pallas import tpu as pltpu
from jax.sharding import PartitionSpec as P

STEPS = 2

time_step = 0.02
bond_scale = 100.0

PLANES, ROWS = 10, 16
LOW = 3
V, K, D, FIELD_COUNT = 3, 6, 7, 13
ROLLS = (-2, -1, 1, 2)


def bond_offsets():
    table = []
    for step_x in range(0, 4):
        for step_y in range(-3, 4):
            for step_z in range(-3, 4):
                if step_x * step_x + step_y * step_y + step_z * step_z <= 9 and (
                    step_x,
                    step_y,
                    step_z,
                ) > (0, 0, 0):
                    table.append((step_x, step_y, step_z))
    return table


BONDS = list(enumerate(bond_offsets()))

RIGHT_WORDS = [(3, 2, w) for w in range(1, 6)] + [(2, 1, w) for w in range(3, 6)]
X_TILES = 12 + len(RIGHT_WORDS)


def y_slots(upward):
    slots = []
    place = 0

    def put(kind, comp, depth, plane, count):
        nonlocal place
        here = LOW + 7 - depth if upward else LOW + depth
        there = LOW - 1 - depth if upward else LOW + 8 + depth
        slots.append((kind, comp, here, there, plane, count, place))
        place += count

    for kind, comps in (("u", 3), ("s", 1)):
        for comp in range(comps):
            for depth in range(3):
                put(kind, comp, depth, *((1, 8) if depth < 2 else (3, 4)))
    for comp in range(3):
        for depth in range(3):
            put("d", comp, depth, 3, 4)
    words = ((0, 1, 2, 3, 4, 5), (0, 1, 3, 5), (1,)) if upward else ((1, 2, 3, 4), (1, 3))
    for depth, row_words in enumerate(words):
        for word in row_words:
            put("w", word, depth, *((3, 4) if upward and word < 2 else (1, 6)))
    return slots, place


UP_SLOTS, UP_ROWS = y_slots(True)
DOWN_SLOTS, DOWN_ROWS = y_slots(False)
Y_ROWS = -(-max(UP_ROWS, DOWN_ROWS) // 8) * 8

CORNER_ROWS = (1, 2, 11, 12)


def line_of(row):
    return {0: 0, 1: 1, 2: 2, 11: 3, 12: 4, 13: 5, 3: 0, 4: 1, 5: 2, 8: 3, 9: 4, 10: 5}[row]


def spot(ref, plane, row, count=8):
    if ref.shape[-2] == ROWS:
        return (plane, slice(row, row + count))
    return (slice(plane * ROWS + row, plane * ROWS + row + count),)


def rolled(value, distance):
    return pltpu.roll(value, (-distance) % 128, value.ndim - 1)


def lane_mask(distance):
    lane = lax.broadcasted_iota(jnp.int32, (8, 128), 1)
    return lane < 128 - distance if distance > 0 else lane >= -distance


def roll_field(source, target, planes, halves=(0, 8)):
    for c in range(3):
        for plane in planes:
            for half in halves:
                value = source[(c,) + spot(source, plane, half)]
                for i, ez in enumerate(ROLLS):
                    target[(c, i) + spot(target, plane, half)] = rolled(value, ez)


def roll_stiffness(source, target, planes, halves=(0, 8)):
    for plane in planes:
        for half in halves:
            value = source[spot(source, plane, half)]
            for i, ez in enumerate(ROLLS):
                moved = jnp.where(lane_mask(ez), rolled(value, ez), 0.0)
                target[(i,) + spot(target, plane, half)] = moved


def add_bond(total, source, target, length, weight):
    sep = [a - b for a, b in zip(source, target)]
    square = sep[0] * sep[0] + sep[1] * sep[1] + sep[2] * sep[2]
    factor = (1.0 / length - lax.rsqrt(square)) * weight
    return [t + factor * p for t, p in zip(total, sep)]


def intact(q, words, value):
    return jnp.where(jnp.bitwise_and(words, 1 << (q % 11)) == 0, value, 0.0)


def rolled_back(part, ez):
    mask = lane_mask(-ez)
    return [jnp.where(mask, rolled(p, -ez), 0.0) for p in part]


def accumulate(plane, base, owned, reacted, u, ur, s, sr, d):
    here = [u[(c,) + spot(u, plane, base)] for c in range(3)]
    total = [jnp.zeros((8, 128), jnp.float32) for _ in range(3)]

    for ez in range(-3, 4):
        for q, (ex, ey, _) in [b for b in owned if b[1][2] == ez]:
            row, at = base + ey, plane + ex
            length = math.sqrt(ex * ex + ey * ey + ez * ez)
            if ez == 0:
                source = [u[(c,) + spot(u, at, row)] for c in range(3)]
                stiff = s[spot(s, at, row)]
            elif abs(ez) < 3:
                i = ROLLS.index(ez)
                source = [ur[(c, i) + spot(ur, at, row)] for c in range(3)]
                stiff = sr[(i,) + spot(sr, at, row)]
            else:
                source = [rolled(h, ez) for h in here]
                stiff = jnp.where(lane_mask(ez), rolled(s[spot(s, at, row)], ez), 0.0)
            target = [h - float(e) for h, e in zip(here, (ex, ey, ez))]
            words = d[(q // 11,) + spot(d, plane, base)]
            total = add_bond(total, source, target, length, intact(q, words, stiff))
        bonds = [b for b in reacted if b[1][2] == ez]
        if not bonds:
            continue
        moved = here if ez == 0 else [rolled(h, ez) for h in here]
        part = total if ez == 0 else [jnp.zeros((8, 128), jnp.float32) for _ in range(3)]
        for q, (ex, ey, _) in bonds:
            row, at = base - ey, plane - ex
            length = math.sqrt(ex * ex + ey * ey + ez * ez)
            source = [u[(c,) + spot(u, at, row)] for c in range(3)]
            target = [h + float(e) for h, e in zip(moved, (ex, ey, ez))]
            stiff = s[spot(s, at, row)]
            words = d[(q // 11,) + spot(d, at, row)]
            part = add_bond(part, source, target, length, intact(q, words, stiff))
        if ez == 0:
            total = part
        else:
            total = [t + p for t, p in zip(total, rolled_back(part, ez))]
    return total


def accumulate_row(row, sources, u, d, other):
    ou, our, os, osr, od, odr = other

    def line(plain, turned, lead, ez, plane, at):
        ref, lead = (plain, lead) if ez == 0 else (turned, lead + (ROLLS.index(ez),))
        return ref[lead + (line_of(at), slice(plane, plane + 8))]

    here = [u[c, line_of(row), 2:10] for c in range(3)]
    total = [jnp.zeros((8, 128), jnp.float32) for _ in range(3)]
    for q, bond in BONDS:
        length = math.sqrt(sum(e * e for e in bond))
        for sign in (1, -1):
            ex, ey, ez = (sign * e for e in bond)
            if row + ey not in sources:
                continue
            plane, at = 2 + ex, row + ey
            source = [line(ou, our, (c,), ez, plane, at) for c in range(3)]
            stiff = line(os, osr, (), ez, plane, at)
            if sign > 0:
                word = d[q // 11, line_of(row), 2:10]
            else:
                word = line(od, odr, (q // 11,), ez, plane, at)
            target = [h - float(e) for h, e in zip(here, (ex, ey, ez))]
            total = add_bond(total, source, target, length, intact(q, word, stiff))
    return [part[0:4] for part in total]


def put_own(fields, u, s, d):
    for x in range(4):
        if u is not None:
            for c in range(3):
                u[(c,) + spot(u, x + 3, LOW)] = fields[c, x]
        if s is not None:
            s[spot(s, x + 3, LOW)] = jnp.sqrt(fields[K, x])
        for w in range(6):
            d[(w,) + spot(d, x + 3, LOW)] = fields[D + w, x].astype(jnp.int32)


def put_zeros(ref, leads, planes, row, count):
    for lead in leads:
        for plane in planes:
            ref[lead + spot(ref, plane, row, count)] = jnp.zeros((count, 128), ref.dtype)


def put_sides(even, near, far, u, s, d):
    rows = slice(LOW, LOW + 8)

    def left(i):
        return jnp.where(even, far[i], near[i])

    def right(i):
        return jnp.where(even, near[i], far[i])

    for plane in range(3):
        for c in range(3):
            if u is not None:
                u[(c,) + spot(u, plane, LOW)] = left(3 * c + plane)
                u[(c,) + spot(u, 7 + plane, LOW)] = right(3 * c + plane)
        s[spot(s, plane, LOW)] = jnp.sqrt(left(9 + plane))
        s[spot(s, 7 + plane, LOW)] = jnp.sqrt(right(9 + plane))
    for i, (_, plane, word) in enumerate(RIGHT_WORDS):
        d[(word,) + spot(d, plane, LOW)] = left(12 + i).astype(jnp.int32)
    d[(5,) + spot(d, 0, LOW)] = jnp.zeros((8, 128), jnp.int32)


def message_lines(even, a, b):
    for slots, above in ((DOWN_SLOTS, True), (UP_SLOTS, False)):
        for slot in slots:
            place, count = slot[6], slot[5]
            one, two = a[place : place + count], b[place : place + count]
            yield slot, jnp.where(even, one, two) if above else jnp.where(even, two, one)


def put_lines(even, a, b, u, s, d, edge):
    for (kind, comp, _, there, plane, count, _), value in message_lines(even, a, b):
        at, planes = line_of(there), slice(plane - 1, plane - 1 + count)
        if kind == "u":
            u[comp, at, planes] = value
        elif kind == "s":
            s[at, planes] = value
        elif kind == "d":
            edge[comp, at, 0:4] = value
        else:
            d[comp, at, planes] = value.astype(jnp.int32)


def put_rows(even, a, b, s, d, wanted):
    for (kind, comp, _, there, plane, count, _), value in message_lines(even, a, b):
        for i in range(count):
            if (plane + i in wanted) and kind == "s":
                s[spot(s, plane + i, there, 1)] = value[i : i + 1]
            elif (plane + i in wanted) and kind == "w":
                d[(comp,) + spot(d, plane + i, there, 1)] = value[i : i + 1].astype(jnp.int32)


def even_place():
    return tuple(lax.axis_index(axis) % 2 == 0 for axis in ("gx", "gy"))


def joined_fields(displacement, velocity, stiffness, damage):
    parts = (displacement, velocity, stiffness[None], damage)
    total, before = 0.0, 0
    for part in parts:
        count = part.shape[0]
        widths = ((before, FIELD_COUNT - before - count, 0),) + ((0, 0, 0),) * 3
        total = total + lax.pad(part, part.dtype.type(0), widths).astype(jnp.float32)
        before += count
    return total


def pack_x(fields, far, near):
    even, _ = even_place()
    for i, field in enumerate((0, 1, 2, K)):
        for plane in range(3):
            one, two = fields[field, plane + 1], fields[field, plane]
            if field == K and plane == 0:
                ((q, _),) = [b for b in BONDS if b[1][0] == 3]
                one = intact(q, fields[D + q // 11, 1].astype(jnp.int32), one)
            near[3 * i + plane] = jnp.where(even, one, two)
            far[3 * i + plane] = jnp.where(even, two, one)
    for i, (plane, _, word) in enumerate(RIGHT_WORDS):
        near[12 + i] = fields[D + word, plane]
        far[12 + i] = fields[D + word, plane]


SIDES = (0, 1, 2, 7, 8, 9)
OUTER = ((0, LOW), (LOW + 8, ROWS - LOW - 8))
EACH = ((0,), (1,), (2,))


def own_part(u, ur, s, sr, d, force):
    roll_field(u, ur, range(3, 7))
    roll_stiffness(s, sr, range(3, 7))
    for i in range(4):
        for plane in (7, 8):
            put_zeros(ur, [(c, i) for c in range(3)], (plane,), 0, ROWS)
            put_zeros(sr, [(i,)], (plane,), 0, ROWS)

    @pl.loop(0, 4)
    def _(x):
        total = accumulate(x + 3, LOW, BONDS, BONDS, u, ur, s, sr, d)
        for c in range(3):
            force[c, x] = total[c]


def side_part(x, u, ur, s, sr, d):
    owned = [b for b in BONDS if x + b[1][0] > 3]
    reacted = [b for b in BONDS if x - b[1][0] < 0]
    return accumulate(x + 3, LOW, owned, reacted, u, ur, s, sr, d)


def first_own(fields, force, u, ur, s, sr, d):
    put_zeros(u, EACH, SIDES, 0, ROWS)
    put_zeros(s, [()], SIDES, 0, ROWS)
    for row, count in OUTER:
        put_zeros(u, EACH, range(3, 7), row, count)
        put_zeros(s, [()], range(3, 7), row, count)
        put_zeros(d, [(w,) for w in range(6)], range(3, 7), row, count)
    put_own(fields, u, s, d)
    own_part(u, ur, s, sr, d, force)


def first_sides(fields, far_x, near_x, force, b, a, v_part, u, ur, s, sr, d, near, up, down):
    even_x, even = even_place()
    for row, count in OUTER:
        put_zeros(u, EACH, SIDES, row, count)
        put_zeros(s, [()], SIDES, row, count)
    put_own(fields, u, s, d)
    put_sides(even_x, near_x, far_x, u, s, d)
    for row, count in OUTER:
        put_zeros(ur, [(c, i) for c in range(3) for i in range(4)], (7, 8), row, count)
        put_zeros(sr, [(i,) for i in range(4)], (7, 8), row, count)
    roll_field(u, ur, (7, 8), (LOW,))
    roll_stiffness(s, sr, (7, 8), (LOW,))
    for x in range(4):
        total = side_part(x, u, ur, s, sr, d)
        scale = bond_scale * s[spot(s, x + 3, LOW)]
        for c in range(3):
            velocity = fields[V + c, x] + time_step * (scale * (force[c, x] + total[c]))
            v_part[c, x] = velocity
            near[(c,) + spot(u, x + 3, LOW)] = fields[c, x] + time_step * velocity

    for slots, message in ((UP_SLOTS, up), (DOWN_SLOTS, down)):
        for kind, comp, here, _, plane, count, place in slots:
            lines = pl.ds(plane * ROWS + here, count, stride=ROWS)
            if kind == "u":
                value = u[comp, lines]
            elif kind == "s":
                value = s[lines]
            elif kind == "d":
                value = near[comp, lines]
            else:
                value = d[comp, lines].astype(jnp.float32)
            message[place : place + count] = value
    a[...] = jnp.where(even, up[...], down[...])
    b[...] = jnp.where(even, down[...], up[...])


def roll_lines(u, ur, s, sr, d, dr, words):
    for at in range(6):
        if not words[at]:
            continue
        for i, ez in enumerate(ROLLS):
            for w in words[at]:
                dr[w, i, at, 0:8] = rolled(d[w, at, 0:8], ez)
            for c in range(3):
                ur[c, i, at, 0:8] = rolled(u[c, at, 0:8], ez)
            sr[i, at, 0:8] = jnp.where(lane_mask(ez), rolled(s[at, 0:8], ez), 0.0)


def second_own(fields, far_x, near_x, u, ur, s, sr, d, dr, whole_u, whole_s, whole_d):
    even_x, _ = even_place()
    put_own(fields, whole_u, whole_s, whole_d)
    put_sides(even_x, near_x, far_x, whole_u, whole_s, whole_d)
    for row in (3, 4, 5, 8, 9, 10):
        at, lines = line_of(row), pl.ds(ROWS + row, 8, stride=ROWS)
        for c in range(3):
            u[c, at, 0:8] = whole_u[c, lines]
        s[at, 0:8] = whole_s[lines]
        for w in range(6):
            d[w, at, 0:8] = whole_d[w, lines]
    roll_lines(u, ur, s, sr, d, dr, [range(6)] * 6)


def second_rows(fields, b, a, v_part, u, ur, s, sr, d, dr, v_out, near, edge, to_far, to_near, hu, hur, hs, hsr, hd, hdr, sums):
    even_x, even = even_place()
    put_lines(even, a, b, hu, hs, hd, edge)
    sent = UP_SLOTS + DOWN_SLOTS
    words = [[k[1] for k in sent if k[0] == "w" and line_of(k[3]) == at] for at in range(6)]
    words[0] = words[5] = []
    roll_lines(hu, hur, hs, hsr, hd, hdr, words)
    beside = (u, ur, s, sr, d, dr)
    beyond = (hu, hur, hs, hsr, hd, hdr)
    for row in (3, 4, 5, 8, 9, 10):
        sources = range(0, LOW) if row < LOW + 4 else range(LOW + 8, LOW + 11)
        force = accumulate_row(row, sources, u, d, beyond)
        for c in range(3):
            sums[c, 8 * (row - LOW) : 8 * (row - LOW) + 4] = force[c]
    for c in range(3):
        for row in (6, 7):
            sums[c, 8 * (row - LOW) : 8 * (row - LOW) + 8] = jnp.zeros((8, 128), jnp.float32)
    for row in (0, 1, 2, 11, 12, 13):
        sources = range(LOW, LOW + 3) if row < LOW + 4 else range(LOW + 5, LOW + 8)
        force = accumulate_row(row, sources, hu, hd, beside)
        at = line_of(row)
        scale = (time_step * time_step * bond_scale) * hs[at, 2:6]
        for c in range(3):
            edge[c, at, 0:4] += scale * force[c]
    for x in range(4):
        scale = (time_step * bond_scale) * jnp.sqrt(fields[K, x])
        for c in range(3):
            velocity = v_part[c, x] + scale * sums[c, pl.ds(x, 8, stride=8)]
            v_out[c, x] = velocity
            near[c, x] = fields[c, x] + time_step * velocity

    place = 0
    for c in range(3):
        for plane in range(3):
            one, two = near[c, plane + 1], near[c, plane]
            to_near[place : place + 8] = jnp.where(even_x, one, two)
            to_far[place : place + 8] = jnp.where(even_x, two, one)
            place += 8
    for c in range(3):
        for row in CORNER_ROWS:
            one, two = edge[c, line_of(row), 2:4], edge[c, line_of(row), 0:2]
            to_near[place : place + 2] = jnp.where(even_x, one, two)
            to_far[place : place + 2] = jnp.where(even_x, two, one)
            place += 2


def last_own(fields, far_x, near_x, b, a, near, edge, force, s, sr, d, u, ur):
    even_x, even = even_place()
    put_zeros(u, EACH, SIDES, 0, ROWS)
    put_zeros(s, [()], SIDES, 0, ROWS)
    put_own(fields, None, s, d)
    put_rows(even, a, b, s, d, range(3, 7))
    for c in range(3):
        u[c, 3:7, LOW : LOW + 8] = near[c]
        for row in (0, 1, 2, 11, 12, 13):
            for x in range(4):
                u[c, x + 3, row : row + 1] = edge[c, line_of(row), x : x + 1]
    own_part(u, ur, s, sr, d, force)
    put_sides(even_x, near_x, far_x, None, s, d)
    put_rows(even, a, b, s, d, SIDES)
    roll_stiffness(s, sr, (7, 8))


def last_sides(near, v_in, force, s, sr, d, far_u, near_u, u_out, v_out, u, ur):
    even_x, _ = even_place()
    for c in range(3):
        u[c, 3:7, LOW : LOW + 8] = near[c]
    put_zeros(u, EACH, SIDES, 0, LOW)
    put_zeros(u, EACH, SIDES, LOW + 8, ROWS - LOW - 8)
    place = 0
    for c in range(3):
        for plane in range(3):
            one, two = near_u[place : place + 8], far_u[place : place + 8]
            u[c, plane, LOW : LOW + 8] = jnp.where(even_x, two, one)
            u[c, 7 + plane, LOW : LOW + 8] = jnp.where(even_x, one, two)
            place += 8
    for c in range(3):
        for row in CORNER_ROWS:
            one, two = near_u[place : place + 2], far_u[place : place + 2]
            before, behind = jnp.where(even_x, two, one), jnp.where(even_x, one, two)
            for plane in range(2):
                u[c, 1 + plane, row : row + 1] = before[plane : plane + 1]
                u[c, 7 + plane, row : row + 1] = behind[plane : plane + 1]
            place += 2
    roll_field(u, ur, (7, 8))
    for x in range(4):
        total = side_part(x, u, ur, s, sr, d)
        scale = bond_scale * s[x + 3, LOW : LOW + 8]
        for c in range(3):
            velocity = v_in[c, x] + time_step * (scale * (force[c, x] + total[c]))
            v_out[c, x] = velocity
            u_out[c, x] = near[c, x] + time_step * velocity


def f32(*shape):
    return jax.ShapeDtypeStruct(shape, jnp.float32)


def arrays(*tail):
    shapes = [f32(3, *tail), f32(3, 4, *tail), f32(*tail), f32(4, *tail)]
    return shapes + [jax.ShapeDtypeStruct((6,) + tail, jnp.int32)]


LAYERS = arrays(PLANES, ROWS, 128)
FLAT = arrays(PLANES * ROWS, 128)
LINES = arrays(6, 16, 128) + [jax.ShapeDtypeStruct((6, 4, 6, 16, 128), jnp.int32)]


def scratch(shapes):
    return [pltpu.VMEM(s.shape, s.dtype) for s in shapes]


def call(kernel, outputs, buffers, *operands, flops=1000):
    return pl.pallas_call(
        kernel,
        out_shape=outputs,
        in_specs=[pl.BlockSpec(memory_space=pltpu.VMEM)] * len(operands),
        out_specs=[pl.BlockSpec(memory_space=pltpu.VMEM)] * len(outputs),
        scratch_shapes=scratch(buffers),
        compiler_params=pltpu.CompilerParams(vmem_limit_bytes=32 * 1024 * 1024),
        cost_estimate=pl.CostEstimate(flops=flops, bytes_accessed=flops, transcendentals=0),
    )(*operands)


def swapped(value, axis, first):
    pairs = [(i, i + 1) for i in range(first, lax.axis_size(axis) - 1, 2)]
    return lax.ppermute(value, axis, pairs + [(j, i) for i, j in pairs])


def shards(displacement, velocity, stiffness, damage):
    point = f32(3, 4, 8, 128)
    edge = f32(3, 6, 8, 128)
    fields = joined_fields(displacement, velocity, stiffness, damage)
    far_x, near_x = call(pack_x, [f32(X_TILES, 8, 128)] * 2, [], fields)
    far_x = swapped(far_x, "gx", 1)
    near_x = swapped(near_x, "gx", 0)
    (force,) = call(first_own, [point], LAYERS, fields, flops=4_000_000)
    message = f32(Y_ROWS, 128)
    b, a, v_part = call(
        first_sides, [message, message, point], FLAT + [FLAT[0], message, message], fields, far_x, near_x, force
    )
    b = swapped(b, "gy", 1)
    a = swapped(a, "gy", 0)
    lines = call(second_own, LINES, [FLAT[0], FLAT[2], FLAT[4]], fields, far_x, near_x, flops=2_000_000)
    velocity, near, edge, far_u, near_u = call(
        second_rows,
        [point, point, edge, f32(96, 128), f32(96, 128)],
        LINES + [f32(3, 64, 128)],
        fields,
        b,
        a,
        v_part,
        *lines,
    )
    kept = (fields, far_x, near_x, b, a, near, edge)
    far_u = swapped(far_u.reshape(12, 8, 128), "gx", 1).reshape(96, 128)
    near_u = swapped(near_u.reshape(12, 8, 128), "gx", 0).reshape(96, 128)
    force, *stiff = call(last_own, [point] + LAYERS[2:], LAYERS[:2], *kept, flops=4_000_000)
    return tuple(
        call(last_sides, [point, point], LAYERS[:2], near, velocity, force, *stiff, far_u, near_u)
    )


def solution(mesh):
    return jax.shard_map(
        shards,
        mesh=mesh,
        in_specs=(
            P(None, "gx", "gy", None),
            P(None, "gx", "gy", None),
            P("gx", "gy", None),
            P(None, "gx", "gy", None),
        ),
        out_specs=(P(None, "gx", "gy", None), P(None, "gx", "gy", None)),
        check_vma=False,
    )
```

```python
import math

import jax
import jax.numpy as jnp
from jax import lax
from jax.experimental import pallas as pl
from jax.experimental.pallas import tpu as pltpu
from jax.sharding import PartitionSpec as P

STEPS = 2

time_step = 0.02
bond_scale = 100.0

PLANES, ROWS = 10, 16
LOW = 3
K, D, FIELD_COUNT = 3, 4, 10
ROLLS = (-2, -1, 1, 2)


def bond_offsets():
    table = []
    for step_x in range(0, 4):
        for step_y in range(-3, 4):
            for step_z in range(-3, 4):
                if step_x * step_x + step_y * step_y + step_z * step_z <= 9 and (
                    step_x,
                    step_y,
                    step_z,
                ) > (0, 0, 0):
                    table.append((step_x, step_y, step_z))
    return table


BONDS = list(enumerate(bond_offsets()))

RIGHT_WORDS = [(3, 2, w) for w in range(1, 6)] + [(2, 1, w) for w in range(3, 6)]
X_TILES = 12 + len(RIGHT_WORDS)


def y_slots(upward):
    slots = []
    place = 0

    def put(kind, comp, depth, plane, count):
        nonlocal place
        here = LOW + 7 - depth if upward else LOW + depth
        there = LOW - 1 - depth if upward else LOW + 8 + depth
        slots.append((kind, comp, here, there, plane, count, place))
        place += count

    for kind, comps in (("u", 3), ("s", 1)):
        for comp in range(comps):
            for depth in range(3):
                put(kind, comp, depth, *((1, 8) if depth < 2 else (3, 4)))
    for comp in range(3):
        for depth in range(3):
            put("d", comp, depth, 3, 4)
    words = ((0, 1, 2, 3, 4, 5), (0, 1, 3, 5), (1,)) if upward else ((1, 2, 3, 4), (1, 3))
    for depth, row_words in enumerate(words):
        for word in row_words:
            put("w", word, depth, *((3, 4) if upward and word < 2 else (1, 6)))
    return slots, place


UP_SLOTS, UP_ROWS = y_slots(True)
DOWN_SLOTS, DOWN_ROWS = y_slots(False)
Y_ROWS = -(-max(UP_ROWS, DOWN_ROWS) // 8) * 8

CORNER_ROWS = (1, 2, 11, 12)


def line_of(row):
    return {0: 0, 1: 1, 2: 2, 11: 3, 12: 4, 13: 5, 3: 0, 4: 1, 5: 2, 8: 3, 9: 4, 10: 5}[row]


def spot(ref, plane, row, count=8):
    if ref.shape[-2] == ROWS:
        return (plane, slice(row, row + count))
    return (slice(plane * ROWS + row, plane * ROWS + row + count),)


def rolled(value, distance):
    return pltpu.roll(value, (-distance) % 128, value.ndim - 1)


def lane_mask(distance):
    lane = lax.broadcasted_iota(jnp.int32, (8, 128), 1)
    return lane < 128 - distance if distance > 0 else lane >= -distance


def roll_field(source, target, planes, halves=(0, 8)):
    for c in range(3):
        for plane in planes:
            for half in halves:
                value = source[(c,) + spot(source, plane, half)]
                for i, ez in enumerate(ROLLS):
                    target[(c, i) + spot(target, plane, half)] = rolled(value, ez)


def roll_stiffness(source, target, planes, halves=(0, 8)):
    for plane in planes:
        for half in halves:
            value = source[spot(source, plane, half)]
            for i, ez in enumerate(ROLLS):
                moved = jnp.where(lane_mask(ez), rolled(value, ez), 0.0)
                target[(i,) + spot(target, plane, half)] = moved


def add_bond(total, source, target, length, weight):
    sep = [a - b for a, b in zip(source, target)]
    square = sep[0] * sep[0] + sep[1] * sep[1] + sep[2] * sep[2]
    factor = (1.0 / length - lax.rsqrt(square)) * weight
    return [t + factor * p for t, p in zip(total, sep)]


def intact(q, words, value):
    return jnp.where(jnp.bitwise_and(words, 1 << (q % 11)) == 0, value, 0.0)


def rolled_back(part, ez):
    mask = lane_mask(-ez)
    return [jnp.where(mask, rolled(p, -ez), 0.0) for p in part]


def accumulate(plane, base, owned, reacted, u, ur, s, sr, d):
    here = [u[(c,) + spot(u, plane, base)] for c in range(3)]
    total = [jnp.zeros((8, 128), jnp.float32) for _ in range(3)]

    for ez in range(-3, 4):
        for q, (ex, ey, _) in [b for b in owned if b[1][2] == ez]:
            row, at = base + ey, plane + ex
            length = math.sqrt(ex * ex + ey * ey + ez * ez)
            if ez == 0:
                source = [u[(c,) + spot(u, at, row)] for c in range(3)]
                stiff = s[spot(s, at, row)]
            elif abs(ez) < 3:
                i = ROLLS.index(ez)
                source = [ur[(c, i) + spot(ur, at, row)] for c in range(3)]
                stiff = sr[(i,) + spot(sr, at, row)]
            else:
                source = [rolled(h, ez) for h in here]
                stiff = jnp.where(lane_mask(ez), rolled(s[spot(s, at, row)], ez), 0.0)
            target = [h - float(e) for h, e in zip(here, (ex, ey, ez))]
            words = d[(q // 11,) + spot(d, plane, base)]
            total = add_bond(total, source, target, length, intact(q, words, stiff))
        bonds = [b for b in reacted if b[1][2] == ez]
        if not bonds:
            continue
        moved = here if ez == 0 else [rolled(h, ez) for h in here]
        part = total if ez == 0 else [jnp.zeros((8, 128), jnp.float32) for _ in range(3)]
        for q, (ex, ey, _) in bonds:
            row, at = base - ey, plane - ex
            length = math.sqrt(ex * ex + ey * ey + ez * ez)
            source = [u[(c,) + spot(u, at, row)] for c in range(3)]
            target = [h + float(e) for h, e in zip(moved, (ex, ey, ez))]
            stiff = s[spot(s, at, row)]
            words = d[(q // 11,) + spot(d, at, row)]
            part = add_bond(part, source, target, length, intact(q, words, stiff))
        if ez == 0:
            total = part
        else:
            total = [t + p for t, p in zip(total, rolled_back(part, ez))]
    return total


def accumulate_row(row, sources, u, d, other):
    ou, our, os, osr, od, odr = other

    def line(plain, turned, lead, ez, plane, at):
        ref, lead = (plain, lead) if ez == 0 else (turned, lead + (ROLLS.index(ez),))
        return ref[lead + (line_of(at), slice(plane, plane + 8))]

    here = [u[c, line_of(row), 2:10] for c in range(3)]
    total = [jnp.zeros((8, 128), jnp.float32) for _ in range(3)]
    for q, bond in BONDS:
        length = math.sqrt(sum(e * e for e in bond))
        for sign in (1, -1):
            ex, ey, ez = (sign * e for e in bond)
            if row + ey not in sources:
                continue
            plane, at = 2 + ex, row + ey
            source = [line(ou, our, (c,), ez, plane, at) for c in range(3)]
            stiff = line(os, osr, (), ez, plane, at)
            if sign > 0:
                word = d[q // 11, line_of(row), 2:10]
            else:
                word = line(od, odr, (q // 11,), ez, plane, at)
            target = [h - float(e) for h, e in zip(here, (ex, ey, ez))]
            total = add_bond(total, source, target, length, intact(q, word, stiff))
    return [part[0:4] for part in total]


def put_own(fields, u, s, d):
    for x in range(4):
        if u is not None:
            for c in range(3):
                u[(c,) + spot(u, x + 3, LOW)] = fields[c, x]
        if s is not None:
            s[spot(s, x + 3, LOW)] = jnp.sqrt(fields[K, x])
        for w in range(6):
            d[(w,) + spot(d, x + 3, LOW)] = fields[D + w, x].astype(jnp.int32)


def put_zeros(ref, leads, planes, row, count):
    for lead in leads:
        for plane in planes:
            ref[lead + spot(ref, plane, row, count)] = jnp.zeros((count, 128), ref.dtype)


def put_sides(even, near, far, u, s, d):
    rows = slice(LOW, LOW + 8)

    def left(i):
        return jnp.where(even, far[i], near[i])

    def right(i):
        return jnp.where(even, near[i], far[i])

    for plane in range(3):
        for c in range(3):
            if u is not None:
                u[(c,) + spot(u, plane, LOW)] = left(3 * c + plane)
                u[(c,) + spot(u, 7 + plane, LOW)] = right(3 * c + plane)
        s[spot(s, plane, LOW)] = jnp.sqrt(left(9 + plane))
        s[spot(s, 7 + plane, LOW)] = jnp.sqrt(right(9 + plane))
    for i, (_, plane, word) in enumerate(RIGHT_WORDS):
        d[(word,) + spot(d, plane, LOW)] = left(12 + i).astype(jnp.int32)
    d[(5,) + spot(d, 0, LOW)] = jnp.zeros((8, 128), jnp.int32)


def message_lines(even, a, b):
    for slots, above in ((DOWN_SLOTS, True), (UP_SLOTS, False)):
        for slot in slots:
            place, count = slot[6], slot[5]
            one, two = a[place : place + count], b[place : place + count]
            yield slot, jnp.where(even, one, two) if above else jnp.where(even, two, one)


def put_lines(even, a, b, u, s, d, edge):
    for (kind, comp, _, there, plane, count, _), value in message_lines(even, a, b):
        at, planes = line_of(there), slice(plane - 1, plane - 1 + count)
        if kind == "u":
            u[comp, at, planes] = value
        elif kind == "s":
            s[at, planes] = value
        elif kind == "d":
            edge[comp, at, 0:4] = value
        else:
            d[comp, at, planes] = value.astype(jnp.int32)


def put_rows(even, a, b, s, d, wanted):
    for (kind, comp, _, there, plane, count, _), value in message_lines(even, a, b):
        for i in range(count):
            if (plane + i in wanted) and kind == "s":
                s[spot(s, plane + i, there, 1)] = value[i : i + 1]
            elif (plane + i in wanted) and kind == "w":
                d[(comp,) + spot(d, plane + i, there, 1)] = value[i : i + 1].astype(jnp.int32)


def even_place():
    return tuple(lax.axis_index(axis) % 2 == 0 for axis in ("gx", "gy"))


def joined_fields(displacement, stiffness, damage):
    parts = (displacement, stiffness[None], damage)
    total, before = 0.0, 0
    for part in parts:
        count = part.shape[0]
        widths = ((before, FIELD_COUNT - before - count, 0),) + ((0, 0, 0),) * 3
        total = total + lax.pad(part, part.dtype.type(0), widths).astype(jnp.float32)
        before += count
    return total


def pack_x(fields, far, near):
    even, _ = even_place()
    for i, field in enumerate((0, 1, 2, K)):
        for plane in range(3):
            one, two = fields[field, plane + 1], fields[field, plane]
            if field == K and plane == 0:
                ((q, _),) = [b for b in BONDS if b[1][0] == 3]
                one = intact(q, fields[D + q // 11, 1].astype(jnp.int32), one)
            near[3 * i + plane] = jnp.where(even, one, two)
            far[3 * i + plane] = jnp.where(even, two, one)
    for i, (plane, _, word) in enumerate(RIGHT_WORDS):
        near[12 + i] = fields[D + word, plane]
        far[12 + i] = fields[D + word, plane]


SIDES = (0, 1, 2, 7, 8, 9)
OUTER = ((0, LOW), (LOW + 8, ROWS - LOW - 8))
EACH = ((0,), (1,), (2,))


def own_part(u, ur, s, sr, d, force):
    roll_field(u, ur, range(3, 7))
    roll_stiffness(s, sr, range(3, 7))
    for i in range(4):
        for plane in (7, 8):
            put_zeros(ur, [(c, i) for c in range(3)], (plane,), 0, ROWS)
            put_zeros(sr, [(i,)], (plane,), 0, ROWS)

    @pl.loop(0, 4)
    def _(x):
        total = accumulate(x + 3, LOW, BONDS, BONDS, u, ur, s, sr, d)
        for c in range(3):
            force[c, x] = total[c]


def side_part(x, u, ur, s, sr, d):
    owned = [b for b in BONDS if x + b[1][0] > 3]
    reacted = [b for b in BONDS if x - b[1][0] < 0]
    return accumulate(x + 3, LOW, owned, reacted, u, ur, s, sr, d)


def first_own(fields, v_in, force, v_kept, u, ur, s, sr, d):
    v_kept[...] = v_in[...]
    put_zeros(u, EACH, SIDES, 0, ROWS)
    put_zeros(s, [()], SIDES, 0, ROWS)
    for row, count in OUTER:
        put_zeros(u, EACH, range(3, 7), row, count)
        put_zeros(s, [()], range(3, 7), row, count)
        put_zeros(d, [(w,) for w in range(6)], range(3, 7), row, count)
    put_own(fields, u, s, d)
    own_part(u, ur, s, sr, d, force)


def first_sides(fields, v_in, far_x, near_x, force, b, a, v_part, u, ur, s, sr, d, near, up, down):
    even_x, even = even_place()
    for row, count in OUTER:
        put_zeros(u, EACH, SIDES, row, count)
        put_zeros(s, [()], SIDES, row, count)
    put_own(fields, u, s, d)
    put_sides(even_x, near_x, far_x, u, s, d)
    for row, count in OUTER:
        put_zeros(ur, [(c, i) for c in range(3) for i in range(4)], (7, 8), row, count)
        put_zeros(sr, [(i,) for i in range(4)], (7, 8), row, count)
    roll_field(u, ur, (7, 8), (LOW,))
    roll_stiffness(s, sr, (7, 8), (LOW,))
    for x in range(4):
        total = side_part(x, u, ur, s, sr, d)
        scale = bond_scale * s[spot(s, x + 3, LOW)]
        for c in range(3):
            velocity = v_in[c, x] + time_step * (scale * (force[c, x] + total[c]))
            v_part[c, x] = velocity
            near[(c,) + spot(u, x + 3, LOW)] = fields[c, x] + time_step * velocity

    for slots, message in ((UP_SLOTS, up), (DOWN_SLOTS, down)):
        for kind, comp, here, _, plane, count, place in slots:
            lines = pl.ds(plane * ROWS + here, count, stride=ROWS)
            if kind == "u":
                value = u[comp, lines]
            elif kind == "s":
                value = s[lines]
            elif kind == "d":
                value = near[comp, lines]
            else:
                value = d[comp, lines].astype(jnp.float32)
            message[place : place + count] = value
    a[...] = jnp.where(even, up[...], down[...])
    b[...] = jnp.where(even, down[...], up[...])


def roll_lines(u, ur, s, sr, d, dr, words):
    for at in range(6):
        if not words[at]:
            continue
        for i, ez in enumerate(ROLLS):
            for w in words[at]:
                dr[w, i, at, 0:8] = rolled(d[w, at, 0:8], ez)
            for c in range(3):
                ur[c, i, at, 0:8] = rolled(u[c, at, 0:8], ez)
            sr[i, at, 0:8] = jnp.where(lane_mask(ez), rolled(s[at, 0:8], ez), 0.0)


def second_own(fields, far_x, near_x, u, ur, s, sr, d, dr, whole_u, whole_s, whole_d):
    even_x, _ = even_place()
    put_own(fields, whole_u, whole_s, whole_d)
    put_sides(even_x, near_x, far_x, whole_u, whole_s, whole_d)
    for row in (3, 4, 5, 8, 9, 10):
        at, lines = line_of(row), pl.ds(ROWS + row, 8, stride=ROWS)
        for c in range(3):
            u[c, at, 0:8] = whole_u[c, lines]
        s[at, 0:8] = whole_s[lines]
        for w in range(6):
            d[w, at, 0:8] = whole_d[w, lines]
    roll_lines(u, ur, s, sr, d, dr, [range(6)] * 6)


def second_rows(fields, b, a, v_part, u, ur, s, sr, d, dr, v_out, near, edge, to_far, to_near, hu, hur, hs, hsr, hd, hdr, sums):
    even_x, even = even_place()
    put_lines(even, a, b, hu, hs, hd, edge)
    sent = UP_SLOTS + DOWN_SLOTS
    words = [[k[1] for k in sent if k[0] == "w" and line_of(k[3]) == at] for at in range(6)]
    words[0] = words[5] = []
    roll_lines(hu, hur, hs, hsr, hd, hdr, words)
    beside = (u, ur, s, sr, d, dr)
    beyond = (hu, hur, hs, hsr, hd, hdr)
    for row in (3, 4, 5, 8, 9, 10):
        sources = range(0, LOW) if row < LOW + 4 else range(LOW + 8, LOW + 11)
        force = accumulate_row(row, sources, u, d, beyond)
        for c in range(3):
            sums[c, 8 * (row - LOW) : 8 * (row - LOW) + 4] = force[c]
    for c in range(3):
        for row in (6, 7):
            sums[c, 8 * (row - LOW) : 8 * (row - LOW) + 8] = jnp.zeros((8, 128), jnp.float32)
    for row in (0, 1, 2, 11, 12, 13):
        sources = range(LOW, LOW + 3) if row < LOW + 4 else range(LOW + 5, LOW + 8)
        force = accumulate_row(row, sources, hu, hd, beside)
        at = line_of(row)
        scale = (time_step * time_step * bond_scale) * hs[at, 2:6]
        for c in range(3):
            edge[c, at, 0:4] += scale * force[c]
    for x in range(4):
        scale = (time_step * bond_scale) * jnp.sqrt(fields[K, x])
        for c in range(3):
            velocity = v_part[c, x] + scale * sums[c, pl.ds(x, 8, stride=8)]
            v_out[c, x] = velocity
            near[c, x] = fields[c, x] + time_step * velocity

    place = 0
    for c in range(3):
        for plane in range(3):
            one, two = near[c, plane + 1], near[c, plane]
            to_near[place : place + 8] = jnp.where(even_x, one, two)
            to_far[place : place + 8] = jnp.where(even_x, two, one)
            place += 8
    for c in range(3):
        for row in CORNER_ROWS:
            one, two = edge[c, line_of(row), 2:4], edge[c, line_of(row), 0:2]
            to_near[place : place + 2] = jnp.where(even_x, one, two)
            to_far[place : place + 2] = jnp.where(even_x, two, one)
            place += 2


def last_own(fields, far_x, near_x, b, a, near, edge, force, s, sr, d, u, ur):
    even_x, even = even_place()
    put_zeros(u, EACH, SIDES, 0, ROWS)
    put_zeros(s, [()], SIDES, 0, ROWS)
    put_own(fields, None, s, d)
    put_rows(even, a, b, s, d, range(3, 7))
    for c in range(3):
        u[c, 3:7, LOW : LOW + 8] = near[c]
        for row in (0, 1, 2, 11, 12, 13):
            for x in range(4):
                u[c, x + 3, row : row + 1] = edge[c, line_of(row), x : x + 1]
    own_part(u, ur, s, sr, d, force)
    put_sides(even_x, near_x, far_x, None, s, d)
    put_rows(even, a, b, s, d, SIDES)
    roll_stiffness(s, sr, (7, 8))


def last_sides(near, v_in, force, s, sr, d, far_u, near_u, u_out, v_out, u, ur):
    even_x, _ = even_place()
    for c in range(3):
        u[c, 3:7, LOW : LOW + 8] = near[c]
    put_zeros(u, EACH, SIDES, 0, LOW)
    put_zeros(u, EACH, SIDES, LOW + 8, ROWS - LOW - 8)
    place = 0
    for c in range(3):
        for plane in range(3):
            one, two = near_u[place : place + 8], far_u[place : place + 8]
            u[c, plane, LOW : LOW + 8] = jnp.where(even_x, two, one)
            u[c, 7 + plane, LOW : LOW + 8] = jnp.where(even_x, one, two)
            place += 8
    for c in range(3):
        for row in CORNER_ROWS:
            one, two = near_u[place : place + 2], far_u[place : place + 2]
            before, behind = jnp.where(even_x, two, one), jnp.where(even_x, one, two)
            for plane in range(2):
                u[c, 1 + plane, row : row + 1] = before[plane : plane + 1]
                u[c, 7 + plane, row : row + 1] = behind[plane : plane + 1]
            place += 2
    roll_field(u, ur, (7, 8))
    for x in range(4):
        total = side_part(x, u, ur, s, sr, d)
        scale = bond_scale * s[x + 3, LOW : LOW + 8]
        for c in range(3):
            velocity = v_in[c, x] + time_step * (scale * (force[c, x] + total[c]))
            v_out[c, x] = velocity
            u_out[c, x] = near[c, x] + time_step * velocity


def f32(*shape):
    return jax.ShapeDtypeStruct(shape, jnp.float32)


def arrays(*tail):
    shapes = [f32(3, *tail), f32(3, 4, *tail), f32(*tail), f32(4, *tail)]
    return shapes + [jax.ShapeDtypeStruct((6,) + tail, jnp.int32)]


LAYERS = arrays(PLANES, ROWS, 128)
FLAT = arrays(PLANES * ROWS, 128)
LINES = arrays(6, 16, 128) + [jax.ShapeDtypeStruct((6, 4, 6, 16, 128), jnp.int32)]


def scratch(shapes):
    return [pltpu.VMEM(s.shape, s.dtype) for s in shapes]


def call(kernel, outputs, buffers, *operands, flops=1000):
    return pl.pallas_call(
        kernel,
        out_shape=outputs,
        in_specs=[pl.BlockSpec(memory_space=pltpu.VMEM)] * len(operands),
        out_specs=[pl.BlockSpec(memory_space=pltpu.VMEM)] * len(outputs),
        scratch_shapes=scratch(buffers),
        compiler_params=pltpu.CompilerParams(vmem_limit_bytes=32 * 1024 * 1024),
        cost_estimate=pl.CostEstimate(flops=flops, bytes_accessed=flops, transcendentals=0),
    )(*operands)


def swapped(value, axis, first):
    pairs = [(i, i + 1) for i in range(first, lax.axis_size(axis) - 1, 2)]
    return lax.ppermute(value, axis, pairs + [(j, i) for i, j in pairs])


def shards(displacement, velocity, stiffness, damage):
    point = f32(3, 4, 8, 128)
    edge = f32(3, 6, 8, 128)
    fields = joined_fields(displacement, stiffness, damage)
    far_x, near_x = call(pack_x, [f32(X_TILES, 8, 128)] * 2, [], fields)
    far_x = swapped(far_x, "gx", 1)
    near_x = swapped(near_x, "gx", 0)
    force, velocity = call(first_own, [point, point], LAYERS, fields, velocity, flops=4_000_000)
    message = f32(Y_ROWS, 128)
    b, a, v_part = call(
        first_sides, [message, message, point], FLAT + [FLAT[0], message, message], fields, velocity, far_x, near_x, force
    )
    b = swapped(b, "gy", 1)
    a = swapped(a, "gy", 0)
    lines = call(second_own, LINES, [FLAT[0], FLAT[2], FLAT[4]], fields, far_x, near_x, flops=2_000_000)
    velocity, near, edge, far_u, near_u = call(
        second_rows,
        [point, point, edge, f32(96, 128), f32(96, 128)],
        LINES + [f32(3, 64, 128)],
        fields,
        b,
        a,
        v_part,
        *lines,
    )
    kept = (fields, far_x, near_x, b, a, near, edge)
    far_u = swapped(far_u.reshape(12, 8, 128), "gx", 1).reshape(96, 128)
    near_u = swapped(near_u.reshape(12, 8, 128), "gx", 0).reshape(96, 128)
    force, *stiff = call(last_own, [point] + LAYERS[2:], LAYERS[:2], *kept, flops=4_000_000)
    return tuple(
        call(last_sides, [point, point], LAYERS[:2], near, velocity, force, *stiff, far_u, near_u)
    )


def solution(mesh):
    return jax.shard_map(
        shards,
        mesh=mesh,
        in_specs=(
            P(None, "gx", "gy", None),
            P(None, "gx", "gy", None),
            P("gx", "gy", None),
            P(None, "gx", "gy", None),
        ),
        out_specs=(P(None, "gx", "gy", None), P(None, "gx", "gy", None)),
        check_vma=False,
    )
```

```python
import math

import jax
import jax.numpy as jnp
from jax import lax
from jax.experimental import pallas as pl
from jax.experimental.pallas import tpu as pltpu
from jax.sharding import PartitionSpec as P

STEPS = 2

time_step = 0.02
bond_scale = 100.0

PLANES, ROWS = 10, 16
LOW = 3
V, K, D, FIELD_COUNT = 3, 6, 7, 13
ROLLS = (-2, -1, 1, 2)


def bond_offsets():
    table = []
    for step_x in range(0, 4):
        for step_y in range(-3, 4):
            for step_z in range(-3, 4):
                if step_x * step_x + step_y * step_y + step_z * step_z <= 9 and (
                    step_x,
                    step_y,
                    step_z,
                ) > (0, 0, 0):
                    table.append((step_x, step_y, step_z))
    return table


BONDS = list(enumerate(bond_offsets()))

RIGHT_WORDS = [(3, 2, w) for w in range(1, 6)] + [(2, 1, w) for w in range(3, 6)]
X_TILES = 12 + len(RIGHT_WORDS)


def y_slots(upward):
    slots = []
    place = 0

    def put(kind, comp, depth, plane, count):
        nonlocal place
        here = LOW + 7 - depth if upward else LOW + depth
        there = LOW - 1 - depth if upward else LOW + 8 + depth
        slots.append((kind, comp, here, there, plane, count, place))
        place += count

    for kind, comps in (("u", 3), ("s", 1)):
        for comp in range(comps):
            for depth in range(3):
                put(kind, comp, depth, *((1, 8) if depth < 2 else (3, 4)))
    for comp in range(3):
        for depth in range(3):
            put("d", comp, depth, 3, 4)
    words = ((0, 1, 2, 3, 4, 5), (0, 1, 3, 5), (1,)) if upward else ((1, 2, 3, 4), (1, 3))
    for depth, row_words in enumerate(words):
        for word in row_words:
            put("w", word, depth, *((3, 4) if upward and word < 2 else (1, 6)))
    return slots, place


UP_SLOTS, UP_ROWS = y_slots(True)
DOWN_SLOTS, DOWN_ROWS = y_slots(False)
Y_ROWS = -(-max(UP_ROWS, DOWN_ROWS) // 8) * 8

CORNER_ROWS = (1, 2, 11, 12)


def line_of(row):
    return {0: 0, 1: 1, 2: 2, 11: 3, 12: 4, 13: 5, 3: 0, 4: 1, 5: 2, 8: 3, 9: 4, 10: 5}[row]


def spot(ref, plane, row, count=8):
    if ref.shape[-2] == ROWS:
        return (plane, slice(row, row + count))
    return (slice(plane * ROWS + row, plane * ROWS + row + count),)


def rolled(value, distance):
    return pltpu.roll(value, (-distance) % 128, value.ndim - 1)


def lane_mask(distance):
    lane = lax.broadcasted_iota(jnp.int32, (8, 128), 1)
    return lane < 128 - distance if distance > 0 else lane >= -distance


def roll_field(source, target, planes, halves=(0, 8)):
    for c in range(3):
        for plane in planes:
            for half in halves:
                value = source[(c,) + spot(source, plane, half)]
                for i, ez in enumerate(ROLLS):
                    target[(c, i) + spot(target, plane, half)] = rolled(value, ez)


def roll_stiffness(source, target, planes, halves=(0, 8)):
    for plane in planes:
        for half in halves:
            value = source[spot(source, plane, half)]
            for i, ez in enumerate(ROLLS):
                moved = jnp.where(lane_mask(ez), rolled(value, ez), 0.0)
                target[(i,) + spot(target, plane, half)] = moved


def add_bond(total, source, target, length, weight):
    sep = [a - b for a, b in zip(source, target)]
    square = sep[0] * sep[0] + sep[1] * sep[1] + sep[2] * sep[2]
    factor = (1.0 / length - lax.rsqrt(square)) * weight
    return [t + factor * p for t, p in zip(total, sep)]


def intact(q, words, value):
    return jnp.where(jnp.bitwise_and(words, 1 << (q % 11)) == 0, value, 0.0)


def rolled_back(part, ez):
    mask = lane_mask(-ez)
    return [jnp.where(mask, rolled(p, -ez), 0.0) for p in part]


def accumulate(plane, base, owned, reacted, u, ur, s, sr, d, turned):
    here = [u[(c,) + spot(u, plane, base)] for c in range(3)]
    total = [jnp.zeros((8, 128), jnp.float32) for _ in range(3)]

    for ez in range(-3, 4):
        for q, (ex, ey, _) in [b for b in owned if b[1][2] == ez]:
            row, at = base + ey, plane + ex
            length = math.sqrt(ex * ex + ey * ey + ez * ez)
            if ez == 0:
                source = [u[(c,) + spot(u, at, row)] for c in range(3)]
                stiff = s[spot(s, at, row)]
            elif abs(ez) < 3:
                i = ROLLS.index(ez)
                source = [ur[(c, i) + spot(ur, at, row)] for c in range(3)]
                stiff = sr[(i,) + spot(sr, at, row)]
            else:
                source = [rolled(h, ez) for h in here]
                stiff = jnp.where(lane_mask(ez), rolled(s[spot(s, at, row)], ez), 0.0)
            target = [h - float(e) for h, e in zip(here, (ex, ey, ez))]
            words = d[(q // 11,) + spot(d, plane, base)]
            total = add_bond(total, source, target, length, intact(q, words, stiff))
        bonds = [b for b in reacted if b[1][2] == ez]
        if not bonds:
            continue
        if ez == 0:
            moved = here
        elif abs(ez) < 3:
            moved = turned(ROLLS.index(ez))
        else:
            moved = [rolled(h, ez) for h in here]
        part = total if ez == 0 else [jnp.zeros((8, 128), jnp.float32) for _ in range(3)]
        for q, (ex, ey, _) in bonds:
            row, at = base - ey, plane - ex
            length = math.sqrt(ex * ex + ey * ey + ez * ez)
            source = [u[(c,) + spot(u, at, row)] for c in range(3)]
            target = [h + float(e) for h, e in zip(moved, (ex, ey, ez))]
            stiff = s[spot(s, at, row)]
            words = d[(q // 11,) + spot(d, at, row)]
            part = add_bond(part, source, target, length, intact(q, words, stiff))
        if ez == 0:
            total = part
        else:
            total = [t + p for t, p in zip(total, rolled_back(part, ez))]
    return total


def accumulate_row(row, sources, u, d, other):
    ou, our, os, osr, od, odr = other

    def line(plain, turned, lead, ez, plane, at):
        ref, lead = (plain, lead) if ez == 0 else (turned, lead + (ROLLS.index(ez),))
        return ref[lead + (line_of(at), slice(plane, plane + 8))]

    here = [u[c, line_of(row), 2:10] for c in range(3)]
    total = [jnp.zeros((8, 128), jnp.float32) for _ in range(3)]
    for q, bond in BONDS:
        length = math.sqrt(sum(e * e for e in bond))
        for sign in (1, -1):
            ex, ey, ez = (sign * e for e in bond)
            if row + ey not in sources:
                continue
            plane, at = 2 + ex, row + ey
            source = [line(ou, our, (c,), ez, plane, at) for c in range(3)]
            stiff = line(os, osr, (), ez, plane, at)
            if sign > 0:
                word = d[q // 11, line_of(row), 2:10]
            else:
                word = line(od, odr, (q // 11,), ez, plane, at)
            target = [h - float(e) for h, e in zip(here, (ex, ey, ez))]
            total = add_bond(total, source, target, length, intact(q, word, stiff))
    return [part[0:4] for part in total]


def put_own(fields, u, s, d):
    for x in range(4):
        if u is not None:
            for c in range(3):
                u[(c,) + spot(u, x + 3, LOW)] = fields[c, x]
        if s is not None:
            s[spot(s, x + 3, LOW)] = jnp.sqrt(fields[K, x])
        for w in range(6):
            d[(w,) + spot(d, x + 3, LOW)] = fields[D + w, x].astype(jnp.int32)


def put_zeros(ref, leads, planes, row, count):
    for lead in leads:
        for plane in planes:
            ref[lead + spot(ref, plane, row, count)] = jnp.zeros((count, 128), ref.dtype)


def put_sides(even, near, far, u, s, d):
    rows = slice(LOW, LOW + 8)

    def left(i):
        return jnp.where(even, far[i], near[i])

    def right(i):
        return jnp.where(even, near[i], far[i])

    for plane in range(3):
        for c in range(3):
            if u is not None:
                u[(c,) + spot(u, plane, LOW)] = left(3 * c + plane)
                u[(c,) + spot(u, 7 + plane, LOW)] = right(3 * c + plane)
        s[spot(s, plane, LOW)] = jnp.sqrt(left(9 + plane))
        s[spot(s, 7 + plane, LOW)] = jnp.sqrt(right(9 + plane))
    for i, (_, plane, word) in enumerate(RIGHT_WORDS):
        d[(word,) + spot(d, plane, LOW)] = left(12 + i).astype(jnp.int32)
    d[(5,) + spot(d, 0, LOW)] = jnp.zeros((8, 128), jnp.int32)


def message_lines(even, a, b):
    for slots, above in ((DOWN_SLOTS, True), (UP_SLOTS, False)):
        for slot in slots:
            place, count = slot[6], slot[5]
            one, two = a[place : place + count], b[place : place + count]
            yield slot, jnp.where(even, one, two) if above else jnp.where(even, two, one)


def put_lines(even, a, b, u, s, d, edge):
    for (kind, comp, _, there, plane, count, _), value in message_lines(even, a, b):
        at, planes = line_of(there), slice(plane - 1, plane - 1 + count)
        if kind == "u":
            u[comp, at, planes] = value
        elif kind == "s":
            s[at, planes] = value
        elif kind == "d":
            edge[comp, at, 0:4] = value
        else:
            d[comp, at, planes] = value.astype(jnp.int32)


def put_rows(even, a, b, s, d, wanted):
    for (kind, comp, _, there, plane, count, _), value in message_lines(even, a, b):
        for i in range(count):
            if (plane + i in wanted) and kind == "s":
                s[spot(s, plane + i, there, 1)] = value[i : i + 1]
            elif (plane + i in wanted) and kind == "w":
                d[(comp,) + spot(d, plane + i, there, 1)] = value[i : i + 1].astype(jnp.int32)


def even_place():
    return tuple(lax.axis_index(axis) % 2 == 0 for axis in ("gx", "gy"))


def joined_fields(displacement, velocity, stiffness, damage):
    parts = (displacement, velocity, stiffness[None], damage)
    total, before = 0.0, 0
    for part in parts:
        count = part.shape[0]
        widths = ((before, FIELD_COUNT - before - count, 0),) + ((0, 0, 0),) * 3
        total = total + lax.pad(part, part.dtype.type(0), widths).astype(jnp.float32)
        before += count
    return total


def pack_x(fields, far, near):
    even, _ = even_place()
    for i, field in enumerate((0, 1, 2, K)):
        for plane in range(3):
            one, two = fields[field, plane + 1], fields[field, plane]
            if field == K and plane == 0:
                ((q, _),) = [b for b in BONDS if b[1][0] == 3]
                one = intact(q, fields[D + q // 11, 1].astype(jnp.int32), one)
            near[3 * i + plane] = jnp.where(even, one, two)
            far[3 * i + plane] = jnp.where(even, two, one)
    for i, (plane, _, word) in enumerate(RIGHT_WORDS):
        near[12 + i] = fields[D + word, plane]
        far[12 + i] = fields[D + word, plane]


SIDES = (0, 1, 2, 7, 8, 9)
OUTER = ((0, LOW), (LOW + 8, ROWS - LOW - 8))
EACH = ((0,), (1,), (2,))


def own_part(u, ur, s, sr, d, force, kept):
    roll_field(u, ur, range(3, 7))
    roll_stiffness(s, sr, range(3, 7))
    for i in range(4):
        for plane in (7, 8):
            put_zeros(ur, [(c, i) for c in range(3)], (plane,), 0, ROWS)
            put_zeros(sr, [(i,)], (plane,), 0, ROWS)

    for c in range(3):
        for i in range(4):
            for x in range(4):
                kept[c, i, x] = ur[c, i, x + 3, LOW : LOW + 8]

    @pl.loop(0, 4)
    def _(x):
        turned = lambda i: [kept[c, i, x] for c in range(3)]
        total = accumulate(x + 3, LOW, BONDS, BONDS, u, ur, s, sr, d, turned)
        for c in range(3):
            force[c, x] = total[c]


def side_part(x, u, ur, s, sr, d, kept):
    owned = [b for b in BONDS if x + b[1][0] > 3]
    reacted = [b for b in BONDS if x - b[1][0] < 0]
    turned = lambda i: [kept[c, i, x] for c in range(3)]
    return accumulate(x + 3, LOW, owned, reacted, u, ur, s, sr, d, turned)


def first_own(fields, force, kept, u, ur, s, sr, d):
    put_zeros(u, EACH, SIDES, 0, ROWS)
    put_zeros(s, [()], SIDES, 0, ROWS)
    for row, count in OUTER:
        put_zeros(u, EACH, range(3, 7), row, count)
        put_zeros(s, [()], range(3, 7), row, count)
        put_zeros(d, [(w,) for w in range(6)], range(3, 7), row, count)
    put_own(fields, u, s, d)
    own_part(u, ur, s, sr, d, force, kept)


def first_sides(fields, far_x, near_x, force, kept, b, a, v_part, u, ur, s, sr, d, near, up, down):
    even_x, even = even_place()
    for row, count in OUTER:
        put_zeros(u, EACH, SIDES, row, count)
        put_zeros(s, [()], SIDES, row, count)
    put_own(fields, u, s, d)
    put_sides(even_x, near_x, far_x, u, s, d)
    for row, count in OUTER:
        put_zeros(ur, [(c, i) for c in range(3) for i in range(4)], (7, 8), row, count)
        put_zeros(sr, [(i,) for i in range(4)], (7, 8), row, count)
    roll_field(u, ur, (7, 8), (LOW,))
    roll_stiffness(s, sr, (7, 8), (LOW,))
    for x in range(4):
        total = side_part(x, u, ur, s, sr, d, kept)
        scale = bond_scale * s[spot(s, x + 3, LOW)]
        for c in range(3):
            velocity = fields[V + c, x] + time_step * (scale * (force[c, x] + total[c]))
            v_part[c, x] = velocity
            near[(c,) + spot(u, x + 3, LOW)] = fields[c, x] + time_step * velocity

    for slots, message in ((UP_SLOTS, up), (DOWN_SLOTS, down)):
        for kind, comp, here, _, plane, count, place in slots:
            lines = pl.ds(plane * ROWS + here, count, stride=ROWS)
            if kind == "u":
                value = u[comp, lines]
            elif kind == "s":
                value = s[lines]
            elif kind == "d":
                value = near[comp, lines]
            else:
                value = d[comp, lines].astype(jnp.float32)
            message[place : place + count] = value
    a[...] = jnp.where(even, up[...], down[...])
    b[...] = jnp.where(even, down[...], up[...])


def roll_lines(u, ur, s, sr, d, dr, words):
    for at in range(6):
        if not words[at]:
            continue
        for i, ez in enumerate(ROLLS):
            for w in words[at]:
                dr[w, i, at, 0:8] = rolled(d[w, at, 0:8], ez)
            for c in range(3):
                ur[c, i, at, 0:8] = rolled(u[c, at, 0:8], ez)
            sr[i, at, 0:8] = jnp.where(lane_mask(ez), rolled(s[at, 0:8], ez), 0.0)


def second_own(fields, far_x, near_x, u, ur, s, sr, d, dr, whole_u, whole_s, whole_d):
    even_x, _ = even_place()
    put_own(fields, whole_u, whole_s, whole_d)
    put_sides(even_x, near_x, far_x, whole_u, whole_s, whole_d)
    for row in (3, 4, 5, 8, 9, 10):
        at, lines = line_of(row), pl.ds(ROWS + row, 8, stride=ROWS)
        for c in range(3):
            u[c, at, 0:8] = whole_u[c, lines]
        s[at, 0:8] = whole_s[lines]
        for w in range(6):
            d[w, at, 0:8] = whole_d[w, lines]
    roll_lines(u, ur, s, sr, d, dr, [range(6)] * 6)


def second_rows(fields, b, a, v_part, u, ur, s, sr, d, dr, v_out, near, edge, to_far, to_near, hu, hur, hs, hsr, hd, hdr, sums):
    even_x, even = even_place()
    put_lines(even, a, b, hu, hs, hd, edge)
    sent = UP_SLOTS + DOWN_SLOTS
    words = [[k[1] for k in sent if k[0] == "w" and line_of(k[3]) == at] for at in range(6)]
    words[0] = words[5] = []
    roll_lines(hu, hur, hs, hsr, hd, hdr, words)
    beside = (u, ur, s, sr, d, dr)
    beyond = (hu, hur, hs, hsr, hd, hdr)
    for row in (3, 4, 5, 8, 9, 10):
        sources = range(0, LOW) if row < LOW + 4 else range(LOW + 8, LOW + 11)
        force = accumulate_row(row, sources, u, d, beyond)
        for c in range(3):
            sums[c, 8 * (row - LOW) : 8 * (row - LOW) + 4] = force[c]
    for c in range(3):
        for row in (6, 7):
            sums[c, 8 * (row - LOW) : 8 * (row - LOW) + 8] = jnp.zeros((8, 128), jnp.float32)
    for row in (0, 1, 2, 11, 12, 13):
        sources = range(LOW, LOW + 3) if row < LOW + 4 else range(LOW + 5, LOW + 8)
        force = accumulate_row(row, sources, hu, hd, beside)
        at = line_of(row)
        scale = (time_step * time_step * bond_scale) * hs[at, 2:6]
        for c in range(3):
            edge[c, at, 0:4] += scale * force[c]
    for x in range(4):
        scale = (time_step * bond_scale) * jnp.sqrt(fields[K, x])
        for c in range(3):
            velocity = v_part[c, x] + scale * sums[c, pl.ds(x, 8, stride=8)]
            v_out[c, x] = velocity
            near[c, x] = fields[c, x] + time_step * velocity

    place = 0
    for c in range(3):
        for plane in range(3):
            one, two = near[c, plane + 1], near[c, plane]
            to_near[place : place + 8] = jnp.where(even_x, one, two)
            to_far[place : place + 8] = jnp.where(even_x, two, one)
            place += 8
    for c in range(3):
        for row in CORNER_ROWS:
            one, two = edge[c, line_of(row), 2:4], edge[c, line_of(row), 0:2]
            to_near[place : place + 2] = jnp.where(even_x, one, two)
            to_far[place : place + 2] = jnp.where(even_x, two, one)
            place += 2


def last_own(fields, far_x, near_x, b, a, near, edge, force, kept, s, sr, d, u, ur):
    even_x, even = even_place()
    put_zeros(u, EACH, SIDES, 0, ROWS)
    put_zeros(s, [()], SIDES, 0, ROWS)
    put_own(fields, None, s, d)
    put_rows(even, a, b, s, d, range(3, 7))
    for c in range(3):
        u[c, 3:7, LOW : LOW + 8] = near[c]
        for row in (0, 1, 2, 11, 12, 13):
            for x in range(4):
                u[c, x + 3, row : row + 1] = edge[c, line_of(row), x : x + 1]
    own_part(u, ur, s, sr, d, force, kept)
    put_sides(even_x, near_x, far_x, None, s, d)
    put_rows(even, a, b, s, d, SIDES)
    roll_stiffness(s, sr, (7, 8))


def last_sides(near, v_in, force, kept, s, sr, d, far_u, near_u, u_out, v_out, u, ur):
    even_x, _ = even_place()
    for c in range(3):
        u[c, 3:7, LOW : LOW + 8] = near[c]
    put_zeros(u, EACH, SIDES, 0, LOW)
    put_zeros(u, EACH, SIDES, LOW + 8, ROWS - LOW - 8)
    place = 0
    for c in range(3):
        for plane in range(3):
            one, two = near_u[place : place + 8], far_u[place : place + 8]
            u[c, plane, LOW : LOW + 8] = jnp.where(even_x, two, one)
            u[c, 7 + plane, LOW : LOW + 8] = jnp.where(even_x, one, two)
            place += 8
    for c in range(3):
        for row in CORNER_ROWS:
            one, two = near_u[place : place + 2], far_u[place : place + 2]
            before, behind = jnp.where(even_x, two, one), jnp.where(even_x, one, two)
            for plane in range(2):
                u[c, 1 + plane, row : row + 1] = before[plane : plane + 1]
                u[c, 7 + plane, row : row + 1] = behind[plane : plane + 1]
            place += 2
    roll_field(u, ur, (7, 8))
    for x in range(4):
        total = side_part(x, u, ur, s, sr, d, kept)
        scale = bond_scale * s[x + 3, LOW : LOW + 8]
        for c in range(3):
            velocity = v_in[c, x] + time_step * (scale * (force[c, x] + total[c]))
            v_out[c, x] = velocity
            u_out[c, x] = near[c, x] + time_step * velocity


def f32(*shape):
    return jax.ShapeDtypeStruct(shape, jnp.float32)


def arrays(*tail):
    shapes = [f32(3, *tail), f32(3, 4, *tail), f32(*tail), f32(4, *tail)]
    return shapes + [jax.ShapeDtypeStruct((6,) + tail, jnp.int32)]


LAYERS = arrays(PLANES, ROWS, 128)
FLAT = arrays(PLANES * ROWS, 128)
LINES = arrays(6, 16, 128) + [jax.ShapeDtypeStruct((6, 4, 6, 16, 128), jnp.int32)]


def scratch(shapes):
    return [pltpu.VMEM(s.shape, s.dtype) for s in shapes]


def call(kernel, outputs, buffers, *operands, flops=1000):
    return pl.pallas_call(
        kernel,
        out_shape=outputs,
        in_specs=[pl.BlockSpec(memory_space=pltpu.VMEM)] * len(operands),
        out_specs=[pl.BlockSpec(memory_space=pltpu.VMEM)] * len(outputs),
        scratch_shapes=scratch(buffers),
        compiler_params=pltpu.CompilerParams(vmem_limit_bytes=32 * 1024 * 1024),
        cost_estimate=pl.CostEstimate(flops=flops, bytes_accessed=flops, transcendentals=0),
    )(*operands)


def swapped(value, axis, first):
    pairs = [(i, i + 1) for i in range(first, lax.axis_size(axis) - 1, 2)]
    return lax.ppermute(value, axis, pairs + [(j, i) for i, j in pairs])


def shards(displacement, velocity, stiffness, damage):
    point = f32(3, 4, 8, 128)
    edge = f32(3, 6, 8, 128)
    fields = joined_fields(displacement, velocity, stiffness, damage)
    far_x, near_x = call(pack_x, [f32(X_TILES, 8, 128)] * 2, [], fields)
    far_x = swapped(far_x, "gx", 1)
    near_x = swapped(near_x, "gx", 0)
    turned = f32(3, 4, 4, 8, 128)
    force, kept = call(first_own, [point, turned], LAYERS, fields, flops=4_000_000)
    message = f32(Y_ROWS, 128)
    b, a, v_part = call(
        first_sides, [message, message, point], FLAT + [FLAT[0], message, message], fields, far_x, near_x, force, kept
    )
    b = swapped(b, "gy", 1)
    a = swapped(a, "gy", 0)
    lines = call(second_own, LINES, [FLAT[0], FLAT[2], FLAT[4]], fields, far_x, near_x, flops=2_000_000)
    velocity, near, edge, far_u, near_u = call(
        second_rows,
        [point, point, edge, f32(96, 128), f32(96, 128)],
        LINES + [f32(3, 64, 128)],
        fields,
        b,
        a,
        v_part,
        *lines,
    )
    kept = (fields, far_x, near_x, b, a, near, edge)
    far_u = swapped(far_u.reshape(12, 8, 128), "gx", 1).reshape(96, 128)
    near_u = swapped(near_u.reshape(12, 8, 128), "gx", 0).reshape(96, 128)
    force, *stiff = call(last_own, [point, turned] + LAYERS[2:], LAYERS[:2], *kept, flops=4_000_000)
    return tuple(
        call(last_sides, [point, point], LAYERS[:2], near, velocity, force, *stiff, far_u, near_u)
    )


def solution(mesh):
    return jax.shard_map(
        shards,
        mesh=mesh,
        in_specs=(
            P(None, "gx", "gy", None),
            P(None, "gx", "gy", None),
            P("gx", "gy", None),
            P(None, "gx", "gy", None),
        ),
        out_specs=(P(None, "gx", "gy", None), P(None, "gx", "gy", None)),
        check_vma=False,
    )
```

```python
import math

import jax
import jax.numpy as jnp
from jax import lax
from jax.experimental import pallas as pl
from jax.experimental.pallas import tpu as pltpu
from jax.sharding import PartitionSpec as P

STEPS = 2

time_step = 0.02
bond_scale = 100.0

PLANES, ROWS = 10, 16
LOW = 3
V, K, D, FIELD_COUNT = 3, 6, 7, 13
ROLLS = (-2, -1, 1, 2)


def bond_offsets():
    table = []
    for step_x in range(0, 4):
        for step_y in range(-3, 4):
            for step_z in range(-3, 4):
                if step_x * step_x + step_y * step_y + step_z * step_z <= 9 and (
                    step_x,
                    step_y,
                    step_z,
                ) > (0, 0, 0):
                    table.append((step_x, step_y, step_z))
    return table


BONDS = list(enumerate(bond_offsets()))

RIGHT_WORDS = [(3, 2, w) for w in range(1, 6)] + [(2, 1, w) for w in range(3, 6)]
X_TILES = 12 + len(RIGHT_WORDS)


def y_slots(upward):
    slots = []
    place = 0

    def put(kind, comp, depth, plane, count):
        nonlocal place
        here = LOW + 7 - depth if upward else LOW + depth
        there = LOW - 1 - depth if upward else LOW + 8 + depth
        slots.append((kind, comp, here, there, plane, count, place))
        place += count

    for kind, comps in (("u", 3), ("s", 1)):
        for comp in range(comps):
            for depth in range(3):
                put(kind, comp, depth, *((1, 8) if depth < 2 else (3, 4)))
    for comp in range(3):
        for depth in range(3):
            put("d", comp, depth, 3, 4)
    words = ((0, 1, 2, 3, 4, 5), (0, 1, 3, 5), (1,)) if upward else ((1, 2, 3, 4), (1, 3))
    for depth, row_words in enumerate(words):
        for word in row_words:
            put("w", word, depth, *((3, 4) if upward and word < 2 else (1, 6)))
    return slots, place


UP_SLOTS, UP_ROWS = y_slots(True)
DOWN_SLOTS, DOWN_ROWS = y_slots(False)
Y_ROWS = -(-max(UP_ROWS, DOWN_ROWS) // 8) * 8

CORNER_ROWS = (1, 2, 11, 12)


def line_of(row):
    return {0: 0, 1: 1, 2: 2, 11: 3, 12: 4, 13: 5, 3: 0, 4: 1, 5: 2, 8: 3, 9: 4, 10: 5}[row]


def spot(ref, plane, row, count=8):
    if ref.shape[-2] == ROWS:
        return (plane, slice(row, row + count))
    return (slice(plane * ROWS + row, plane * ROWS + row + count),)


def rolled(value, distance):
    return pltpu.roll(value, (-distance) % 128, value.ndim - 1)


def lane_mask(distance):
    lane = lax.broadcasted_iota(jnp.int32, (8, 128), 1)
    return lane < 128 - distance if distance > 0 else lane >= -distance


def roll_field(source, target, planes, halves=(0, 8)):
    for c in range(3):
        for plane in planes:
            for half in halves:
                value = source[(c,) + spot(source, plane, half)]
                for i, ez in enumerate(ROLLS):
                    target[(c, i) + spot(target, plane, half)] = rolled(value, ez)


def roll_stiffness(source, target, planes, halves=(0, 8)):
    for plane in planes:
        for half in halves:
            value = source[spot(source, plane, half)]
            for i, ez in enumerate(ROLLS):
                moved = jnp.where(lane_mask(ez), rolled(value, ez), 0.0)
                target[(i,) + spot(target, plane, half)] = moved


def add_bond(total, source, target, length, weight):
    sep = [a - b for a, b in zip(source, target)]
    square = sep[0] * sep[0] + sep[1] * sep[1] + sep[2] * sep[2]
    factor = (1.0 / length - lax.rsqrt(square)) * weight
    return [t + factor * p for t, p in zip(total, sep)]


def intact(q, words, value):
    return jnp.where(jnp.bitwise_and(words, 1 << (q % 11)) == 0, value, 0.0)


def rolled_back(part, ez):
    mask = lane_mask(-ez)
    return [jnp.where(mask, rolled(p, -ez), 0.0) for p in part]


def accumulate(plane, base, owned, reacted, u, ur, s, sr, d, turned):
    here = [u[(c,) + spot(u, plane, base)] for c in range(3)]
    total = [jnp.zeros((8, 128), jnp.float32) for _ in range(3)]

    for ez in range(-3, 4):
        for q, (ex, ey, _) in [b for b in owned if b[1][2] == ez]:
            row, at = base + ey, plane + ex
            length = math.sqrt(ex * ex + ey * ey + ez * ez)
            if ez == 0:
                source = [u[(c,) + spot(u, at, row)] for c in range(3)]
                stiff = s[spot(s, at, row)]
            elif abs(ez) < 3:
                i = ROLLS.index(ez)
                source = [ur[(c, i) + spot(ur, at, row)] for c in range(3)]
                stiff = sr[(i,) + spot(sr, at, row)]
            else:
                source = [rolled(h, ez) for h in here]
                stiff = jnp.where(lane_mask(ez), rolled(s[spot(s, at, row)], ez), 0.0)
            target = [h - float(e) if e else h for h, e in zip(here, (ex, ey, ez))]
            words = d[(q // 11,) + spot(d, plane, base)]
            total = add_bond(total, source, target, length, intact(q, words, stiff))
        bonds = [b for b in reacted if b[1][2] == ez]
        if not bonds:
            continue
        if ez == 0:
            moved = here
        elif abs(ez) < 3:
            moved = turned(ROLLS.index(ez))
        else:
            moved = [rolled(h, ez) for h in here]
        part = total if ez == 0 else [jnp.zeros((8, 128), jnp.float32) for _ in range(3)]
        for q, (ex, ey, _) in bonds:
            row, at = base - ey, plane - ex
            length = math.sqrt(ex * ex + ey * ey + ez * ez)
            source = [u[(c,) + spot(u, at, row)] for c in range(3)]
            target = [h + float(e) if e else h for h, e in zip(moved, (ex, ey, ez))]
            stiff = s[spot(s, at, row)]
            words = d[(q // 11,) + spot(d, at, row)]
            part = add_bond(part, source, target, length, intact(q, words, stiff))
        if ez == 0:
            total = part
        else:
            total = [t + p for t, p in zip(total, rolled_back(part, ez))]
    return total


def accumulate_row(row, sources, u, d, other):
    ou, our, os, osr, od, odr = other

    def line(plain, turned, lead, ez, plane, at):
        ref, lead = (plain, lead) if ez == 0 else (turned, lead + (ROLLS.index(ez),))
        return ref[lead + (line_of(at), slice(plane, plane + 8))]

    here = [u[c, line_of(row), 2:10] for c in range(3)]
    total = [jnp.zeros((8, 128), jnp.float32) for _ in range(3)]
    for q, bond in BONDS:
        length = math.sqrt(sum(e * e for e in bond))
        for sign in (1, -1):
            ex, ey, ez = (sign * e for e in bond)
            if row + ey not in sources:
                continue
            plane, at = 2 + ex, row + ey
            source = [line(ou, our, (c,), ez, plane, at) for c in range(3)]
            stiff = line(os, osr, (), ez, plane, at)
            if sign > 0:
                word = d[q // 11, line_of(row), 2:10]
            else:
                word = line(od, odr, (q // 11,), ez, plane, at)
            target = [h - float(e) if e else h for h, e in zip(here, (ex, ey, ez))]
            total = add_bond(total, source, target, length, intact(q, word, stiff))
    return [part[0:4] for part in total]


def put_own(fields, u, s, d):
    for x in range(4):
        if u is not None:
            for c in range(3):
                u[(c,) + spot(u, x + 3, LOW)] = fields[c, x]
        if s is not None:
            s[spot(s, x + 3, LOW)] = jnp.sqrt(fields[K, x])
        for w in range(6):
            d[(w,) + spot(d, x + 3, LOW)] = fields[D + w, x].astype(jnp.int32)


def put_zeros(ref, leads, planes, row, count):
    for lead in leads:
        for plane in planes:
            ref[lead + spot(ref, plane, row, count)] = jnp.zeros((count, 128), ref.dtype)


def put_sides(even, near, far, u, s, d):
    rows = slice(LOW, LOW + 8)

    def left(i):
        return jnp.where(even, far[i], near[i])

    def right(i):
        return jnp.where(even, near[i], far[i])

    for plane in range(3):
        for c in range(3):
            if u is not None:
                u[(c,) + spot(u, plane, LOW)] = left(3 * c + plane)
                u[(c,) + spot(u, 7 + plane, LOW)] = right(3 * c + plane)
        s[spot(s, plane, LOW)] = jnp.sqrt(left(9 + plane))
        s[spot(s, 7 + plane, LOW)] = jnp.sqrt(right(9 + plane))
    for i, (_, plane, word) in enumerate(RIGHT_WORDS):
        d[(word,) + spot(d, plane, LOW)] = left(12 + i).astype(jnp.int32)
    d[(5,) + spot(d, 0, LOW)] = jnp.zeros((8, 128), jnp.int32)


def message_lines(even, a, b):
    for slots, above in ((DOWN_SLOTS, True), (UP_SLOTS, False)):
        for slot in slots:
            place, count = slot[6], slot[5]
            one, two = a[place : place + count], b[place : place + count]
            yield slot, jnp.where(even, one, two) if above else jnp.where(even, two, one)


def put_lines(even, a, b, u, s, d, edge):
    for (kind, comp, _, there, plane, count, _), value in message_lines(even, a, b):
        at, planes = line_of(there), slice(plane - 1, plane - 1 + count)
        if kind == "u":
            u[comp, at, planes] = value
        elif kind == "s":
            s[at, planes] = value
        elif kind == "d":
            edge[comp, at, 0:4] = value
        else:
            d[comp, at, planes] = value.astype(jnp.int32)


def put_rows(even, a, b, s, d, wanted):
    for (kind, comp, _, there, plane, count, _), value in message_lines(even, a, b):
        for i in range(count):
            if (plane + i in wanted) and kind == "s":
                s[spot(s, plane + i, there, 1)] = value[i : i + 1]
            elif (plane + i in wanted) and kind == "w":
                d[(comp,) + spot(d, plane + i, there, 1)] = value[i : i + 1].astype(jnp.int32)


def even_place():
    return tuple(lax.axis_index(axis) % 2 == 0 for axis in ("gx", "gy"))


def joined_fields(displacement, velocity, stiffness, damage):
    parts = (displacement, velocity, stiffness[None], damage)
    total, before = 0.0, 0
    for part in parts:
        count = part.shape[0]
        widths = ((before, FIELD_COUNT - before - count, 0),) + ((0, 0, 0),) * 3
        total = total + lax.pad(part, part.dtype.type(0), widths).astype(jnp.float32)
        before += count
    return total


def pack_x(fields, far, near):
    even, _ = even_place()
    for i, field in enumerate((0, 1, 2, K)):
        for plane in range(3):
            one, two = fields[field, plane + 1], fields[field, plane]
            if field == K and plane == 0:
                ((q, _),) = [b for b in BONDS if b[1][0] == 3]
                one = intact(q, fields[D + q // 11, 1].astype(jnp.int32), one)
            near[3 * i + plane] = jnp.where(even, one, two)
            far[3 * i + plane] = jnp.where(even, two, one)
    for i, (plane, _, word) in enumerate(RIGHT_WORDS):
        near[12 + i] = fields[D + word, plane]
        far[12 + i] = fields[D + word, plane]


SIDES = (0, 1, 2, 7, 8, 9)
OUTER = ((0, LOW), (LOW + 8, ROWS - LOW - 8))
EACH = ((0,), (1,), (2,))


def own_part(u, ur, s, sr, d, force, kept):
    roll_field(u, ur, range(3, 7))
    roll_stiffness(s, sr, range(3, 7))
    for i in range(4):
        for plane in (7, 8):
            put_zeros(ur, [(c, i) for c in range(3)], (plane,), 0, ROWS)
            put_zeros(sr, [(i,)], (plane,), 0, ROWS)

    for c in range(3):
        for i in range(4):
            for x in range(4):
                kept[c, i, x] = ur[c, i, x + 3, LOW : LOW + 8]

    @pl.loop(0, 4)
    def _(x):
        turned = lambda i: [kept[c, i, x] for c in range(3)]
        total = accumulate(x + 3, LOW, BONDS, BONDS, u, ur, s, sr, d, turned)
        for c in range(3):
            force[c, x] = total[c]


def side_part(x, u, ur, s, sr, d, kept):
    owned = [b for b in BONDS if x + b[1][0] > 3]
    reacted = [b for b in BONDS if x - b[1][0] < 0]
    turned = lambda i: [kept[c, i, x] for c in range(3)]
    return accumulate(x + 3, LOW, owned, reacted, u, ur, s, sr, d, turned)


def first_own(fields, force, kept, u, ur, s, sr, d):
    put_zeros(u, EACH, SIDES, 0, ROWS)
    put_zeros(s, [()], SIDES, 0, ROWS)
    for row, count in OUTER:
        put_zeros(u, EACH, range(3, 7), row, count)
        put_zeros(s, [()], range(3, 7), row, count)
        put_zeros(d, [(w,) for w in range(6)], range(3, 7), row, count)
    put_own(fields, u, s, d)
    own_part(u, ur, s, sr, d, force, kept)


def first_sides(fields, far_x, near_x, force, kept, b, a, v_part, u, ur, s, sr, d, near, up, down):
    even_x, even = even_place()
    for row, count in OUTER:
        put_zeros(u, EACH, SIDES, row, count)
        put_zeros(s, [()], SIDES, row, count)
    put_own(fields, u, s, d)
    put_sides(even_x, near_x, far_x, u, s, d)
    for row, count in OUTER:
        put_zeros(ur, [(c, i) for c in range(3) for i in range(4)], (7, 8), row, count)
        put_zeros(sr, [(i,) for i in range(4)], (7, 8), row, count)
    roll_field(u, ur, (7, 8), (LOW,))
    roll_stiffness(s, sr, (7, 8), (LOW,))
    for x in range(4):
        total = side_part(x, u, ur, s, sr, d, kept)
        scale = bond_scale * s[spot(s, x + 3, LOW)]
        for c in range(3):
            velocity = fields[V + c, x] + time_step * (scale * (force[c, x] + total[c]))
            v_part[c, x] = velocity
            near[(c,) + spot(u, x + 3, LOW)] = fields[c, x] + time_step * velocity

    for slots, message in ((UP_SLOTS, up), (DOWN_SLOTS, down)):
        for kind, comp, here, _, plane, count, place in slots:
            lines = pl.ds(plane * ROWS + here, count, stride=ROWS)
            if kind == "u":
                value = u[comp, lines]
            elif kind == "s":
                value = s[lines]
            elif kind == "d":
                value = near[comp, lines]
            else:
                value = d[comp, lines].astype(jnp.float32)
            message[place : place + count] = value
    a[...] = jnp.where(even, up[...], down[...])
    b[...] = jnp.where(even, down[...], up[...])


def roll_lines(u, ur, s, sr, d, dr, words):
    for at in range(6):
        if not words[at]:
            continue
        for i, ez in enumerate(ROLLS):
            for w in words[at]:
                dr[w, i, at, 0:8] = rolled(d[w, at, 0:8], ez)
            for c in range(3):
                ur[c, i, at, 0:8] = rolled(u[c, at, 0:8], ez)
            sr[i, at, 0:8] = jnp.where(lane_mask(ez), rolled(s[at, 0:8], ez), 0.0)


def second_own(fields, far_x, near_x, u, ur, s, sr, d, dr, whole_u, whole_s, whole_d):
    even_x, _ = even_place()
    put_own(fields, whole_u, whole_s, whole_d)
    put_sides(even_x, near_x, far_x, whole_u, whole_s, whole_d)
    for row in (3, 4, 5, 8, 9, 10):
        at, lines = line_of(row), pl.ds(ROWS + row, 8, stride=ROWS)
        for c in range(3):
            u[c, at, 0:8] = whole_u[c, lines]
        s[at, 0:8] = whole_s[lines]
        for w in range(6):
            d[w, at, 0:8] = whole_d[w, lines]
    roll_lines(u, ur, s, sr, d, dr, [range(6)] * 6)


def second_rows(fields, b, a, v_part, u, ur, s, sr, d, dr, v_out, near, edge, to_far, to_near, hu, hur, hs, hsr, hd, hdr, sums):
    even_x, even = even_place()
    put_lines(even, a, b, hu, hs, hd, edge)
    sent = UP_SLOTS + DOWN_SLOTS
    words = [[k[1] for k in sent if k[0] == "w" and line_of(k[3]) == at] for at in range(6)]
    words[0] = words[5] = []
    roll_lines(hu, hur, hs, hsr, hd, hdr, words)
    beside = (u, ur, s, sr, d, dr)
    beyond = (hu, hur, hs, hsr, hd, hdr)
    for row in (3, 4, 5, 8, 9, 10):
        sources = range(0, LOW) if row < LOW + 4 else range(LOW + 8, LOW + 11)
        force = accumulate_row(row, sources, u, d, beyond)
        for c in range(3):
            sums[c, 8 * (row - LOW) : 8 * (row - LOW) + 4] = force[c]
    for c in range(3):
        for row in (6, 7):
            sums[c, 8 * (row - LOW) : 8 * (row - LOW) + 8] = jnp.zeros((8, 128), jnp.float32)
    for row in (0, 1, 2, 11, 12, 13):
        sources = range(LOW, LOW + 3) if row < LOW + 4 else range(LOW + 5, LOW + 8)
        force = accumulate_row(row, sources, hu, hd, beside)
        at = line_of(row)
        scale = (time_step * time_step * bond_scale) * hs[at, 2:6]
        for c in range(3):
            edge[c, at, 0:4] += scale * force[c]
    for x in range(4):
        scale = (time_step * bond_scale) * jnp.sqrt(fields[K, x])
        for c in range(3):
            velocity = v_part[c, x] + scale * sums[c, pl.ds(x, 8, stride=8)]
            v_out[c, x] = velocity
            near[c, x] = fields[c, x] + time_step * velocity

    place = 0
    for c in range(3):
        for plane in range(3):
            one, two = near[c, plane + 1], near[c, plane]
            to_near[place : place + 8] = jnp.where(even_x, one, two)
            to_far[place : place + 8] = jnp.where(even_x, two, one)
            place += 8
    for c in range(3):
        for row in CORNER_ROWS:
            one, two = edge[c, line_of(row), 2:4], edge[c, line_of(row), 0:2]
            to_near[place : place + 2] = jnp.where(even_x, one, two)
            to_far[place : place + 2] = jnp.where(even_x, two, one)
            place += 2


def last_own(fields, far_x, near_x, b, a, near, edge, force, kept, s, sr, d, u, ur):
    even_x, even = even_place()
    put_zeros(u, EACH, SIDES, 0, ROWS)
    put_zeros(s, [()], SIDES, 0, ROWS)
    put_own(fields, None, s, d)
    put_rows(even, a, b, s, d, range(3, 7))
    for c in range(3):
        u[c, 3:7, LOW : LOW + 8] = near[c]
        for row in (0, 1, 2, 11, 12, 13):
            for x in range(4):
                u[c, x + 3, row : row + 1] = edge[c, line_of(row), x : x + 1]
    own_part(u, ur, s, sr, d, force, kept)
    put_sides(even_x, near_x, far_x, None, s, d)
    put_rows(even, a, b, s, d, SIDES)
    roll_stiffness(s, sr, (7, 8))


def last_sides(near, v_in, force, kept, s, sr, d, far_u, near_u, u_out, v_out, u, ur):
    even_x, _ = even_place()
    for c in range(3):
        u[c, 3:7, LOW : LOW + 8] = near[c]
    put_zeros(u, EACH, SIDES, 0, LOW)
    put_zeros(u, EACH, SIDES, LOW + 8, ROWS - LOW - 8)
    place = 0
    for c in range(3):
        for plane in range(3):
            one, two = near_u[place : place + 8], far_u[place : place + 8]
            u[c, plane, LOW : LOW + 8] = jnp.where(even_x, two, one)
            u[c, 7 + plane, LOW : LOW + 8] = jnp.where(even_x, one, two)
            place += 8
    for c in range(3):
        for row in CORNER_ROWS:
            one, two = near_u[place : place + 2], far_u[place : place + 2]
            before, behind = jnp.where(even_x, two, one), jnp.where(even_x, one, two)
            for plane in range(2):
                u[c, 1 + plane, row : row + 1] = before[plane : plane + 1]
                u[c, 7 + plane, row : row + 1] = behind[plane : plane + 1]
            place += 2
    roll_field(u, ur, (7, 8))
    for x in range(4):
        total = side_part(x, u, ur, s, sr, d, kept)
        scale = bond_scale * s[x + 3, LOW : LOW + 8]
        for c in range(3):
            velocity = v_in[c, x] + time_step * (scale * (force[c, x] + total[c]))
            v_out[c, x] = velocity
            u_out[c, x] = near[c, x] + time_step * velocity


def f32(*shape):
    return jax.ShapeDtypeStruct(shape, jnp.float32)


def arrays(*tail):
    shapes = [f32(3, *tail), f32(3, 4, *tail), f32(*tail), f32(4, *tail)]
    return shapes + [jax.ShapeDtypeStruct((6,) + tail, jnp.int32)]


LAYERS = arrays(PLANES, ROWS, 128)
FLAT = arrays(PLANES * ROWS, 128)
LINES = arrays(6, 16, 128) + [jax.ShapeDtypeStruct((6, 4, 6, 16, 128), jnp.int32)]


def scratch(shapes):
    return [pltpu.VMEM(s.shape, s.dtype) for s in shapes]


def call(kernel, outputs, buffers, *operands, flops=1000):
    return pl.pallas_call(
        kernel,
        out_shape=outputs,
        in_specs=[pl.BlockSpec(memory_space=pltpu.VMEM)] * len(operands),
        out_specs=[pl.BlockSpec(memory_space=pltpu.VMEM)] * len(outputs),
        scratch_shapes=scratch(buffers),
        compiler_params=pltpu.CompilerParams(vmem_limit_bytes=32 * 1024 * 1024),
        cost_estimate=pl.CostEstimate(flops=flops, bytes_accessed=flops, transcendentals=0),
    )(*operands)


def swapped(value, axis, first):
    pairs = [(i, i + 1) for i in range(first, lax.axis_size(axis) - 1, 2)]
    return lax.ppermute(value, axis, pairs + [(j, i) for i, j in pairs])


def shards(displacement, velocity, stiffness, damage):
    point = f32(3, 4, 8, 128)
    edge = f32(3, 6, 8, 128)
    fields = joined_fields(displacement, velocity, stiffness, damage)
    far_x, near_x = call(pack_x, [f32(X_TILES, 8, 128)] * 2, [], fields)
    far_x = swapped(far_x, "gx", 1)
    near_x = swapped(near_x, "gx", 0)
    turned = f32(3, 4, 4, 8, 128)
    force, kept = call(first_own, [point, turned], LAYERS, fields, flops=4_000_000)
    message = f32(Y_ROWS, 128)
    b, a, v_part = call(
        first_sides, [message, message, point], FLAT + [FLAT[0], message, message], fields, far_x, near_x, force, kept
    )
    b = swapped(b, "gy", 1)
    a = swapped(a, "gy", 0)
    lines = call(second_own, LINES, [FLAT[0], FLAT[2], FLAT[4]], fields, far_x, near_x, flops=2_000_000)
    velocity, near, edge, far_u, near_u = call(
        second_rows,
        [point, point, edge, f32(96, 128), f32(96, 128)],
        LINES + [f32(3, 64, 128)],
        fields,
        b,
        a,
        v_part,
        *lines,
    )
    kept = (fields, far_x, near_x, b, a, near, edge)
    far_u = swapped(far_u.reshape(12, 8, 128), "gx", 1).reshape(96, 128)
    near_u = swapped(near_u.reshape(12, 8, 128), "gx", 0).reshape(96, 128)
    force, *stiff = call(last_own, [point, turned] + LAYERS[2:], LAYERS[:2], *kept, flops=4_000_000)
    return tuple(
        call(last_sides, [point, point], LAYERS[:2], near, velocity, force, *stiff, far_u, near_u)
    )


def solution(mesh):
    return jax.shard_map(
        shards,
        mesh=mesh,
        in_specs=(
            P(None, "gx", "gy", None),
            P(None, "gx", "gy", None),
            P("gx", "gy", None),
            P(None, "gx", "gy", None),
        ),
        out_specs=(P(None, "gx", "gy", None), P(None, "gx", "gy", None)),
        check_vma=False,
    )
```
